32 devices in a mesh: floor: 4 (over x, core), facade: 8 (over z, y).
Axes of the slice: x: 2, y: 2, z: 4, core: 2. Of those that a mesh axis runs over, the one named last changes fastest.
Arguments:
- interface_rhs: float32 [4, 8, 2, 256, 128], P('floor', 'facade'), may hold values from -40 to 40
- inverse_factor: float32 [4, 8, 1024, 1024], P('floor', 'facade')
- near_coupling: bfloat16 [4, 8, 1024, 1024], P('floor', 'facade'), may hold values from -0.09375 to 0.09375
- near_pattern: int32 [4, 8, 8, 8], P('floor', 'facade'), may hold values from 0 to 1, as said below
Outputs:
- multipliers: float32 [4, 8, 2, 256, 128], P('floor', 'facade')
- residual: float32 [4, 8, 2, 256, 128], P('floor', 'facade')
The draws below stay inside these ranges and needn't reach their ends.
Inputs may be any that keep to these rules, and one draw needn't show every extreme that they name: `near_pattern`: every diagonal block is set; each subdomain has from 8 to 32 blocks set, and in every draw some subdomain has exactly 32.
All inputs are finite; a program needn't handle non-finite values.
Results may differ from the reference program's by a relative error of at most 0.0022.
Values sent between devices are 32-bit elements; how exact they have to be, the bound alone decides.
No kernel may reach another device: no remote copies, remote signals or barrier semaphores. Data moves between devices by JAX's collectives and lax.ppermute only.
A program may use at most 64 MiB of HBM per device.

```python
import math
import jax
import jax.numpy as jnp
from jax import lax

FACE = 256
CASES = 128
NB = 8
ITERS = 4
NI = 1024
BLK = 128
MAXB = 32
FLOORS = 4
COLUMNS = 8


def draw_interface_rhs(key, part):
    key_base, key_rows, key_cases = jax.random.split(key, 3)
    full_shape = (FLOORS, COLUMNS, 2, FACE, CASES)
    base_draw = jnp.clip(jax.random.normal(key_base, full_shape, jnp.float32), -5.0, 5.0)
    row_scale = jnp.exp(jax.random.uniform(key_rows, (FLOORS, COLUMNS, 2, FACE, 1), jnp.float32, 0.0, math.log(10.0))) / math.sqrt(10.0)
    case_scale = jnp.exp(jax.random.uniform(key_cases, (1, 1, 1, 1, CASES), jnp.float32, 0.0, math.log(10.0))) / math.sqrt(10.0)
    floor_pos = jnp.arange(FLOORS).reshape(FLOORS, 1, 1, 1, 1)
    column_pos = jnp.arange(COLUMNS).reshape(1, COLUMNS, 1, 1, 1)
    position = (floor_pos * COLUMNS + column_pos).astype(jnp.float32)
    growth = jnp.sqrt(1.0 + 2.0 * position / max(FLOORS * COLUMNS - 1, 1))
    return jnp.clip(base_draw * row_scale * case_scale * growth, -40.0, 40.0)


def draw_inverse_factor(key, part):
    key_diag, key_off = jax.random.split(key)
    full_shape = (FLOORS, COLUMNS, NI, NI)
    diagonal = jax.random.uniform(key_diag, (FLOORS, COLUMNS, NI, 1), jnp.float32, 1.0, 3.0)
    spread = jnp.clip(jax.random.normal(key_off, full_shape, jnp.float32), -5.0, 5.0) * 0.5 / math.sqrt(NI)
    row_index = jnp.arange(NI).reshape(NI, 1)
    col_index = jnp.arange(NI).reshape(1, NI)
    identity = (row_index == col_index).astype(jnp.float32)
    return spread * (1.0 - identity) + identity * diagonal


def draw_near_pattern(key, part):
    key_first, key_second, key_heavy, key_order = jax.random.split(key, 4)
    spare_blocks = MAXB - NB
    first_draw = jax.random.randint(key_first, (FLOORS, COLUMNS), 0, spare_blocks + 1)
    second_draw = jax.random.randint(key_second, (FLOORS, COLUMNS), 0, spare_blocks + 1)
    counts = NB + first_draw * second_draw // max(spare_blocks, 1)
    heavy_device = jax.random.randint(key_heavy, (), 0, FLOORS * COLUMNS)
    flat_index = jnp.arange(FLOORS * COLUMNS).reshape(FLOORS, COLUMNS)
    counts = jnp.where(flat_index == heavy_device, MAXB, counts)
    block_ids = jnp.arange(NB * NB)
    scores = jax.random.randint(key_order, (FLOORS, COLUMNS, NB * NB), 0, 1 << 20) * (NB * NB) + block_ids
    on_diagonal = block_ids // NB == block_ids % NB
    scores = jnp.where(on_diagonal, -1 - block_ids, scores)
    block_rank = jnp.argsort(jnp.argsort(scores, axis=-1), axis=-1)
    live_blocks = (block_rank < counts[:, :, None]).astype(jnp.int32)
    return live_blocks.reshape(FLOORS, COLUMNS, NB, NB)


def levels(stream_key, shape, cuts, smallest, top_value):
    level, own = 1.0, jax.random.fold_in(stream_key, 6)
    for axis_at, blocks in cuts:
        heights = jnp.exp(jax.random.uniform(jax.random.fold_in(own, axis_at), (blocks,), jnp.float32, smallest / len(cuts), top_value / len(cuts)))
        level = level * jnp.repeat(heights, shape[axis_at] // blocks).reshape([-1 if axis == axis_at else 1 for axis in range(len(shape))])
    return level


def bell_draw(stream_key, dims, width, reach, cuts=(), held_as=jnp.bfloat16):
    result = jax.random.normal(stream_key, dims, jnp.float32) * width
    if len(cuts) > 0:
        result = levels(stream_key, dims, cuts, -0.22, 0.18) * result
    return jnp.clip(result, min=-reach, max=reach).astype(held_as)


def setup_inputs(seed: int = 0) -> dict:
    key_list = jax.random.split(jax.random.key(seed), 5)
    return {
        "interface_rhs": draw_interface_rhs(jax.random.fold_in(key_list[4], 71), 0),
        "inverse_factor": draw_inverse_factor(jax.random.fold_in(key_list[4], 71), 0),
        "near_coupling": bell_draw(key_list[2], (FLOORS, COLUMNS, NI, NI), (MAXB * BLK) ** -0.5, 0.09375, ((0, 4), (1, 8))),
        "near_pattern": draw_near_pattern(jax.random.fold_in(key_list[4], 71), 0),
    }


finest = lax.Precision.HIGHEST


def to_trace(owned):
    upper = owned[:, :, 0]
    right_face = owned[:, :, 1]
    below = jnp.concatenate([jnp.zeros_like(upper[:1]), upper[:-1]], axis=0)
    beside = jnp.roll(right_face, 1, axis=1)
    return jnp.stack([-below, upper, -beside, right_face], axis=2)


def from_trace(image, top_keep):
    above = jnp.concatenate([image[1:, :, 0], jnp.zeros_like(image[:1, :, 0])], axis=0)
    beyond = jnp.roll(image[:, :, 2], -1, axis=1)
    upper = (image[:, :, 1] - above) * top_keep
    return jnp.stack([upper, image[:, :, 3] - beyond], axis=2)


def local_floor(operands):
    factor, coupling, pattern, trace_form = operands
    columns = trace_form.shape[0]
    flat = trace_form.reshape(columns, 4 * FACE, CASES)
    inner = jnp.einsum("cij,cjr->cir", factor, flat, precision=finest)
    outer = jnp.einsum("cji,cjr->cir", factor, inner, precision=finest)
    expanded = jnp.repeat(jnp.repeat(pattern, BLK, axis=1), BLK, axis=2)
    masked = coupling.astype(jnp.float32) * expanded.astype(jnp.float32)
    rounded = lax.optimization_barrier(flat.astype(jnp.bfloat16)).astype(jnp.float32)
    forward = jnp.einsum("cij,cjr->cir", masked, rounded, precision=finest)
    forward = lax.optimization_barrier(forward.astype(jnp.bfloat16)).astype(jnp.float32)
    backward = jnp.einsum("cji,cjr->cir", masked, forward, precision=finest)
    return (outer + backward).reshape(columns, 4, FACE, CASES)


def apply_full(owned, inverse_factor, near_coupling, near_pattern, top_keep):
    trace_form = to_trace(owned)
    image = lax.map(local_floor, (inverse_factor, near_coupling, near_pattern, trace_form))
    return from_trace(image, top_keep)


def inner_product(left_side, right_side):
    return jnp.sum(left_side * right_side, axis=(0, 1, 2, 3))


def reference(interface_rhs, inverse_factor, near_coupling, near_pattern):
    top_keep = (jnp.arange(FLOORS) < FLOORS - 1).astype(jnp.float32).reshape(FLOORS, 1, 1, 1)
    rhs = jnp.stack([interface_rhs[:, :, 0] * top_keep, interface_rhs[:, :, 1]], axis=2)
    multipliers = jnp.zeros_like(rhs)
    residual = rhs
    direction = rhs
    norm_now = inner_product(residual, residual)
    for sweep in range(ITERS):
        image = apply_full(direction, inverse_factor, near_coupling, near_pattern, top_keep)
        step_size = norm_now / inner_product(direction, image)
        multipliers = multipliers + step_size * direction
        residual = residual - step_size * image
        norm_next = inner_product(residual, residual)
        direction = residual + (norm_next / norm_now) * direction
        norm_now = norm_next
    return multipliers, residual
```

```python
import functools

import jax
import jax.numpy as jnp
from jax import lax
from jax.experimental import pallas as pl
from jax.experimental.pallas import tpu as pltpu
from jax.sharding import PartitionSpec as P

ITERS = 4
CHUNK = 256
AXES = ("floor", "facade")
F32 = jnp.float32
BF16 = jnp.bfloat16


def halves(x):
    high = x.astype(BF16)
    return high, (x - high.astype(F32)).astype(BF16)


def params(mib):
    return pltpu.CompilerParams(vmem_limit_bytes=mib << 20)


def operator_kernel(pattern, w_ref, n_ref, high_ref, low_ref, total, left, right):
    step = pl.program_id(0)
    size = w_ref.shape[1]
    nb = pattern.shape[0]
    blk = size // nb
    w = w_ref[...]
    high, low = halves(w)
    right[0:CHUNK, :] = high
    right[CHUNK : 2 * CHUNK, :] = low
    right[2 * CHUNK : 3 * CHUNK, :] = high
    for a in range(CHUNK // blk):
        for b in range(nb):
            keep = pattern[step * (CHUNK // blk) + a, b] != 0
            block = n_ref[a * blk : (a + 1) * blk, b * blk : (b + 1) * blk]
            right[3 * CHUNK + a * blk : 3 * CHUNK + (a + 1) * blk, b * blk : (b + 1) * blk] = jnp.where(
                keep, block, jnp.zeros_like(block)
            )
    high_t = high.T
    left[:, 0:CHUNK] = high_t
    left[:, CHUNK : 2 * CHUNK] = high_t
    left[:, 2 * CHUNK : 3 * CHUNK] = low.T
    left[:, 3 * CHUNK : 4 * CHUNK] = right[3 * CHUNK : 4 * CHUNK, :].T

    for i in range(size // CHUNK):
        rows = slice(i * CHUNK, (i + 1) * CHUNK)
        part = jnp.dot(left[rows, :], right[:, i * CHUNK :], preferred_element_type=F32)

        @pl.when(step == 0)
        def _():
            total[rows, i * CHUNK :] = part

        @pl.when(step > 0)
        def _():
            total[rows, i * CHUNK :] += part

    @pl.when(step == pl.num_programs(0) - 1)
    def _():
        for i in range(size // CHUNK):
            for j in range(i, size // CHUNK):
                rows = slice(i * CHUNK, (i + 1) * CHUNK)
                cols = slice(j * CHUNK, (j + 1) * CHUNK)
                block = total[rows, cols]
                high_ref[rows, cols], low_ref[rows, cols] = halves(block)
                if j > i:
                    high_ref[cols, rows], low_ref[cols, rows] = halves(block.T)


def build_operator(factor, coupling, pattern):
    size = factor.shape[0]
    return pl.pallas_call(
        operator_kernel,
        grid=(size // CHUNK,),
        in_specs=[
            pl.BlockSpec(memory_space=pltpu.SMEM),
            pl.BlockSpec((CHUNK, size), lambda k: (k, 0)),
            pl.BlockSpec((CHUNK, size), lambda k: (k, 0)),
        ],
        out_specs=[pl.BlockSpec((size, size), lambda k: (0, 0))] * 2,
        out_shape=[jax.ShapeDtypeStruct((size, size), BF16)] * 2,
        scratch_shapes=[
            pltpu.VMEM((size, size), F32),
            pltpu.VMEM((size, 4 * CHUNK), BF16),
            pltpu.VMEM((4 * CHUNK, size), BF16),
        ],
        compiler_params=params(40),
        name="operator",
    )(pattern, factor, coupling)


def product(high_ref, low_ref, u):
    cases = u.shape[1]
    high, low = halves(u)
    wide = jnp.dot(high_ref[...], jnp.concatenate([high, low], axis=1), preferred_element_type=F32)
    thin = jnp.dot(low_ref[...], high, preferred_element_type=F32)
    return wide[:, :cases] + wide[:, cases:] + thin


def rows_sum(x):
    return jnp.sum(x, axis=0, keepdims=True)


def hand_out(pos, y_ref, outs):
    face = outs[0].shape[0]
    for k, out in enumerate(outs):
        out[...] = y_ref[pl.ds(pl.multiple_of(pos[k] * face, face), face), :]


def take_in(pos, u_ref, own, got):
    face = own[0].shape[0]
    for k in range(4):
        keep = pos[4 + k] != 0
        value = own[k][...] - got[k][...]
        u_ref[pl.ds(pl.multiple_of(pos[k] * face, face), face), :] = jnp.where(keep, value, 0.0)


def first_kernel(pos, below, beside, up, right, high_ref, low_ref, u_ref, a, b, c, d, sums, y_ref):
    face = up.shape[0]
    keep = pos[8] != 0
    u_ref[0:face, :] = -below[...]
    u_ref[face : 2 * face, :] = jnp.where(keep, up[...], 0.0)
    u_ref[2 * face : 3 * face, :] = -beside[...]
    u_ref[3 * face :, :] = right[...]
    u = u_ref[...]
    y = product(high_ref, low_ref, u)
    y_ref[...] = y
    hand_out(pos, y_ref, (a, b, c, d))
    own_up, own_right = u[face : 2 * face], u[3 * face :]
    sums[...] = jnp.zeros_like(sums)
    sums[0:1, :] = rows_sum(own_up * own_up) + rows_sum(own_right * own_right)
    sums[1:2, :] = rows_sum(u * y)


def middle_kernel(pos, ya, yb, yc, yd, ra, rb, rc, rd, high_ref, low_ref, u_ref, a, b, c, d, y_ref):
    take_in(pos, u_ref, (ya, yb, yc, yd), (ra, rb, rc, rd))
    y_ref[...] = product(high_ref, low_ref, u_ref[...])
    hand_out(pos, y_ref, (a, b, c, d))


def last_kernel(
    pos, ya, yb, yc, yd, ra, rb, rc, rd, u0, u1, u2, early, high_ref, low_ref, v1_ref, v2_ref, v3_ref, down, up, left, right, sums, u_ref
):
    take_in(pos, u_ref, (ya, yb, yc, yd), (ra, rb, rc, rd))
    face = down.shape[0]
    scale = early[0:1, :] / early[1:2, :]
    w0 = u0[...]
    w1 = u1[...] * scale
    w2 = u2[...] * scale * scale
    w3 = u_ref[...] * scale * scale * scale
    v1 = w1 - w0
    v2 = w2 - 2.0 * w1 + w0
    v3 = w3 - 3.0 * w2 + 3.0 * w1 - w0
    y = product(high_ref, low_ref, v3)
    down[...] = y[0:face]
    up[...] = y[face : 2 * face]
    left[...] = y[2 * face : 3 * face]
    right[...] = y[3 * face :]

    def owned(x):
        return jnp.concatenate([x[face : 2 * face], x[3 * face :]], axis=0)

    vs = [owned(w0), owned(v1), owned(v2), owned(v3)]
    v1_ref[...] = vs[1]
    v2_ref[...] = vs[2]
    v3_ref[...] = vs[3]
    for m in range(7):
        sums[m : m + 1, :] = rows_sum(vs[m // 2] * vs[(m + 1) // 2])
    sums[7:8, :] = rows_sum(v3 * y)


def conjugate_coefficients(nu):
    def inner(a, b):
        total = None
        for m in range(len(a) + len(b) - 1):
            terms = [a[i] * b[m - i] for i in range(len(a)) if 0 <= m - i < len(b)]
            value = functools.reduce(lambda s, t: s + t, terms) * nu[m]
            total = value if total is None else total + value
        return total

    def plus(a, s, b):
        longer = max(len(a), len(b))
        zero = jnp.zeros_like(nu[0])
        a = a + [zero] * (longer - len(a))
        b = b + [zero] * (longer - len(b))
        return [x + s * y for x, y in zip(a, b)]

    def applied(a):
        zero = jnp.zeros_like(nu[0])
        return [x + y for x, y in zip(a + [zero], [zero] + a)]

    one = jnp.ones_like(nu[0])
    x, r, p = [], [one], [one]
    norm = nu[0]
    for sweep in range(ITERS):
        q = applied(p)
        step = norm / inner(p, q)
        x = plus(x, step, p)
        r = plus(r, -step, q)
        if sweep + 1 < ITERS:
            fresh = inner(r, r)
            p = plus(r, fresh / norm, p)
            norm = fresh
    return x, r


def final_kernel(pos, early, late, u0, v1, v2, v3, yu, yr, gu, gr, mult, resid):
    face = yu.shape[0]
    scale = early[0:1, :] / early[1:2, :]
    nu = [late[m : m + 1, :] for m in range(7)]
    nu.append(late[7:8, :] * scale - nu[6])
    x, r = conjugate_coefficients(nu)
    x = [value * scale for value in x]
    keep = pos[8] != 0
    for f, (own, got) in enumerate(((yu, gu), (yr, gr))):
        rows = slice(f * face, (f + 1) * face)
        w0 = u0[(2 * f + 1) * face : (2 * f + 2) * face, :]
        image = (own[...] - got[...]) * scale
        if f == 0:
            image = jnp.where(keep, image, 0.0)
        v4 = image - v3[rows, :]
        vs = (w0, v1[rows, :], v2[rows, :], v3[rows, :], v4)
        mult[rows, :] = x[0] * vs[0] + x[1] * vs[1] + x[2] * vs[2] + x[3] * vs[3]
        resid[rows, :] = r[0] * vs[0] + r[1] * vs[1] + r[2] * vs[2] + r[3] * vs[3] + r[4] * vs[4]


def upward(value, axis, steps, wrap):
    count = lax.axis_size(axis)
    pairs = [(i, (i + steps) % count) for i in range(count) if wrap or 0 <= i + steps < count]
    return lax.ppermute(value, axis, pairs)


def swapped(value, axis, odd, wrap):
    count = lax.axis_size(axis)
    pairs = []
    for i in range(odd, count, 2):
        if i + 1 < count or wrap:
            j = (i + 1) % count
            pairs += [(i, j), (j, i)]
    return lax.ppermute(value, axis, pairs)


def exchanged(a, b, c, d):
    return (
        swapped(a, "floor", 0, False),
        swapped(b, "floor", 1, False),
        swapped(c, "facade", 0, True),
        swapped(d, "facade", 1, True),
    )


def flipped(value, flip_floor, flip_facade):
    floors, columns = lax.axis_size("floor"), lax.axis_size("facade")
    pairs = [
        (f * columns + c, (f ^ flip_floor) * columns + (c ^ flip_facade)) for f in range(floors) for c in range(columns)
    ]
    return lax.ppermute(value, AXES, pairs)


def sum_stages():
    floors, columns = lax.axis_size("floor"), lax.axis_size("facade")
    flips = []
    bit = 1
    while bit < floors:
        flips.append((bit, 0))
        bit *= 2
    bit = 1
    while bit < columns:
        flips.append((0, bit))
        bit *= 2
    return [flips[:1]] + [flips[k : k + 2] for k in range(1, len(flips), 2)]


def stage_sum(value, stage):
    if len(stage) == 1:
        return value + flipped(value, *stage[0])
    (f1, c1), (f2, c2) = stage
    one, two, both = flipped(value, f1, c1), flipped(value, f2, c2), flipped(value, f1 ^ f2, c1 ^ c2)
    return (value + one) + (two + both)


def whole_sum(value):
    for stage in sum_stages():
        value = stage_sum(value, stage)
    return value


def call(kernel, outs, scratch, *args, smem=1):
    return pl.pallas_call(
        kernel,
        in_specs=[pl.BlockSpec(memory_space=pltpu.SMEM)] * smem
        + [pl.BlockSpec(memory_space=pltpu.VMEM)] * (len(args) - smem),
        out_specs=[pl.BlockSpec(memory_space=pltpu.VMEM)] * len(outs),
        out_shape=outs,
        scratch_shapes=scratch,
        compiler_params=params(32),
    )(*args)


def local(interface_rhs, inverse_factor, near_coupling, near_pattern):
    face, cases = interface_rhs.shape[3:]
    size = 4 * face
    floors = lax.axis_size("floor")
    floor_pos, facade_pos = lax.axis_index("floor"), lax.axis_index("facade")
    odd_floor, odd_facade = floor_pos % 2, facade_pos % 2
    has_below = (floor_pos > 0).astype(jnp.int32)
    has_above = (floor_pos < floors - 1).astype(jnp.int32)
    keep_a = jnp.where(odd_floor == 0, has_above, has_below)
    keep_b = jnp.where(odd_floor == 0, has_below, has_above)
    one = jnp.int32(1)
    pos = jnp.stack(
        [1 - odd_floor, odd_floor, 3 - odd_facade, 2 + odd_facade, keep_a, keep_b, one, one, has_above]
    ).astype(jnp.int32)

    up, right = interface_rhs[0, 0, 0], interface_rhs[0, 0, 1]
    beside = upward(right, "facade", 1, True)
    below = upward(up, "floor", 1, False)
    high, low = build_operator(inverse_factor[0, 0], near_coupling[0, 0], near_pattern[0, 0])

    whole = jax.ShapeDtypeStruct((size, cases), F32)
    part = jax.ShapeDtypeStruct((face, cases), F32)
    owned = jax.ShapeDtypeStruct((2 * face, cases), F32)
    sums = jax.ShapeDtypeStruct((8, cases), F32)
    full = pltpu.VMEM((size, cases), F32)

    u0, *faces, early = call(
        first_kernel, [whole, part, part, part, part, sums], [full], pos, below, beside, up, right, high, low
    )
    early = whole_sum(early)
    us = [u0]
    for _ in range(ITERS - 2):
        u, *faces = call(
            middle_kernel, [whole, part, part, part, part], [full], pos, *faces, *exchanged(*faces), high, low
        )
        us.append(u)
    v1, v2, v3, y_down, y_up, y_left, y_right, late = call(
        last_kernel,
        [owned, owned, owned, part, part, part, part, sums],
        [full],
        pos,
        *faces,
        *exchanged(*faces),
        *us,
        early,
        high,
        low,
    )
    got_right = upward(y_left, "facade", -1, True)
    got_up = upward(y_down, "floor", -1, False)
    late = whole_sum(late)
    mult, resid = call(
        final_kernel, [owned, owned], [], pos, early, late, u0, v1, v2, v3, y_up, y_right, got_up, got_right
    )
    shape = (1, 1, 2, face, cases)
    return mult.reshape(shape), resid.reshape(shape)


def solution(mesh):
    spec = P("floor", "facade", None, None, None)
    flat = P("floor", "facade", None, None)
    return jax.shard_map(
        local,
        mesh=mesh,
        in_specs=(spec, flat, flat, flat),
        out_specs=(spec, spec),
        check_vma=False,
    )
```

```python
import functools

import jax
import jax.numpy as jnp
from jax import lax
from jax.experimental import pallas as pl
from jax.experimental.pallas import tpu as pltpu
from jax.sharding import PartitionSpec as P

ITERS = 4
SLOT, KEEP, ODD = 0, 4, 7
PADS = (8, 0, 24, 16)
PAIRS = [(i, j) for i in range(4) for j in range(i, 4)]
CENTER, NODE = 20, 24
AXES = ("floor", "facade")
F32 = jnp.float32
BF16 = jnp.bfloat16


def halves(x):
    high = x.astype(BF16)
    return high, (x - high.astype(F32)).astype(BF16)


def params(mib):
    return pltpu.CompilerParams(vmem_limit_bytes=mib << 20)


def operator_kernel(info, pattern_hbm, w_hbm, n_hbm, g_ref, center_ref, pattern, w_buf, n_buf, sems, left, right, total):
    size = w_buf.shape[1]
    face = size // 4
    nb = pattern.shape[0]
    blk = size // nb
    pattern_copy = pltpu.make_async_copy(pattern_hbm, pattern, sems.at[2, 0])
    pattern_copy.start()

    def fetch(k):
        rows = pl.ds(k * face, face)
        return (
            pltpu.make_async_copy(w_hbm.at[rows, :], w_buf.at[rows, :], sems.at[0, k]),
            pltpu.make_async_copy(n_hbm.at[rows, :], n_buf.at[rows, :], sems.at[1, k]),
        )

    def prepare(k):
        for copy in fetch(k):
            copy.wait()
        high, low = halves(w_buf[k * face : (k + 1) * face, :])
        here, there = left.at[k % 2], right.at[k % 2]
        there[0:face, :] = high
        there[face : 2 * face, :] = low
        there[2 * face : 3 * face, :] = high
        for a in range(face // blk):
            for b in range(nb):
                keep = pattern[k * (face // blk) + a, b] != 0
                cols = slice(b * blk, (b + 1) * blk)
                block = n_buf[k * face + a * blk : k * face + (a + 1) * blk, cols]
                there[3 * face + a * blk : 3 * face + (a + 1) * blk, cols] = jnp.where(
                    keep, block, jnp.zeros_like(block)
                )
        high_t = high.T
        here[:, 0:face] = high_t
        here[:, face : 2 * face] = high_t
        here[:, 2 * face : 3 * face] = low.T
        here[:, 3 * face :] = there[3 * face :, :].T

    def multiply(k):
        for i in range(4):
            rows, cols = slice(i * face, (i + 1) * face), slice(i * face, size)
            part = jnp.dot(left[k % 2, rows, :], right[k % 2, :, cols], preferred_element_type=F32)
            if k == 0:
                total[rows, cols] = part
            else:
                total[rows, cols] += part

    for k in range(4):
        for copy in fetch(k):
            copy.start()
    pattern_copy.wait()
    prepare(0)
    for k in range(4):
        if k < 3:
            prepare(k + 1)
        multiply(k)

    def put(i, j, block):
        def at(k):
            return pl.multiple_of(info[k] * face, face)

        rows = pl.ds(at(i), face)
        high, low = halves(block)
        g_ref[rows, pl.ds(at(j), face)] = high
        g_ref[rows, pl.ds(pl.multiple_of(size + at(j), face), face)] = low

    diagonal = lax.broadcasted_iota(jnp.int32, (face, face), 0) == lax.broadcasted_iota(jnp.int32, (face, face), 1)
    trace = jnp.zeros((1, face), F32)
    for i in range(4):
        for j in range(i, 4):
            block = total[i * face : (i + 1) * face, j * face : (j + 1) * face]
            put(i, j, block)
            if j == i:
                trace = trace + rows_sum(jnp.where(diagonal, block, 0.0))
            if j > i:
                put(j, i, block.T)


    center_ref[...] = jnp.broadcast_to(jnp.sum(trace, axis=1, keepdims=True) * (2.0 / size), center_ref.shape)


def build_operator(info, factor, coupling, pattern, cases):
    size = factor.shape[0]
    return pl.pallas_call(
        operator_kernel,
        in_specs=[pl.BlockSpec(memory_space=pltpu.SMEM)] + [pl.BlockSpec(memory_space=pl.ANY)] * 3,
        out_specs=[pl.BlockSpec(memory_space=pltpu.VMEM)] * 2,
        out_shape=[jax.ShapeDtypeStruct((size, 2 * size), BF16), jax.ShapeDtypeStruct((8, cases), F32)],
        scratch_shapes=[
            pltpu.SMEM(pattern.shape, jnp.int32),
            pltpu.VMEM((size, size), F32),
            pltpu.VMEM((size, size), BF16),
            pltpu.SemaphoreType.DMA((3, 4)),
            pltpu.VMEM((2, size, size), BF16),
            pltpu.VMEM((2, size, size), BF16),
            pltpu.VMEM((size, size), F32),
        ],
        compiler_params=params(32),
        name="operator",
    )(
        info,
        pltpu.with_memory_space_constraint(pattern, pltpu.HBM),
        pltpu.with_memory_space_constraint(factor, pltpu.HBM),
        pltpu.with_memory_space_constraint(coupling, pltpu.HBM),
    )


def operand(u):
    high, low = halves(u)
    straight = jnp.concatenate([high, low], axis=1)
    crossed = jnp.concatenate([low, high], axis=1)
    return jnp.concatenate([straight, crossed], axis=0)


def product(g_ref, u):
    cases = u.shape[1]
    wide = jnp.dot(g_ref[...], operand(u), preferred_element_type=F32)
    return wide[:, :cases] + wide[:, cases:]


def fine_product(g_ref, u):
    size, cases = u.shape
    high, low = halves(u)
    rest = (u - high.astype(F32) - low.astype(F32)).astype(BF16)
    wide = jnp.dot(g_ref[:, :size], jnp.concatenate([high, low], axis=1), preferred_element_type=F32)
    crossed = jnp.concatenate([jnp.concatenate([rest, jnp.zeros_like(rest)], axis=1), jnp.concatenate([high, low], axis=1)], axis=0)
    fine = jnp.dot(g_ref[...], crossed, preferred_element_type=F32)
    return wide[:, :cases] + (wide[:, cases:] + (fine[:, :cases] + fine[:, cases:]))


def rows_sum(x):
    return jnp.sum(x, axis=0, keepdims=True)


def take_in(info, u_ref, own, got):
    face = u_ref.shape[0] // 4
    for k in range(4):
        value = own[k][0:face, :] - got[k][0:face, :]
        if k < 2:
            value = jnp.where(info[KEEP + k] != 0, value, 0.0)
        u_ref[k * face : (k + 1) * face, :] = value


def hand_out(y, outs):
    face = y.shape[0] // 4
    for k, out in enumerate(outs):
        out[0:face, :] = y[k * face : (k + 1) * face]
        if out.shape[0] > face:
            out[face:, :] = jnp.zeros((out.shape[0] - face, out.shape[1]), F32)


def first_kernel(info, below, beside, up, right, g_ref, u_ref, a, b, c, d):
    face = up.shape[0]
    own_up = jnp.where(info[KEEP + 2] != 0, up[...], 0.0)
    own_right = right[...]
    odd_floor, odd_facade = info[ODD] != 0, info[ODD + 1] != 0
    u_ref[0:face, :] = jnp.where(odd_floor, -below[...], own_up)
    u_ref[face : 2 * face, :] = jnp.where(odd_floor, own_up, -below[...])
    u_ref[2 * face : 3 * face, :] = jnp.where(odd_facade, -beside[...], own_right)
    u_ref[3 * face :, :] = jnp.where(odd_facade, own_right, -beside[...])
    hand_out(product(g_ref, u_ref[...]), (a, b, c, d))


def next_kernel(fine, info, ya, yb, yc, yd, ra, rb, rc, rd, g_ref, u_ref, a, b, c, d):
    take_in(info, u_ref, (ya, yb, yc, yd), (ra, rb, rc, rd))
    hand_out((fine_product if fine else product)(g_ref, u_ref[...]), (a, b, c, d))


def differences(w, scale):
    values = []
    power = None
    for k, value in enumerate(w):
        values.append(value if k == 0 else value * power)
        power = scale if k == 0 else power * scale
    out = [values[0]]
    while len(values) > 1:
        values = [values[k + 1] - values[k] for k in range(len(values) - 1)]
        out.append(values[0])
    return out


def last_kernel(info, ya, yb, yc, yd, ra, rb, rc, rd, u0, u1, u2, *rest):
    ys, (center, g_ref, u_ref, down, left, yo_ref, node, y_ref) = rest[:8], rest[8:]
    ys = [ys[:4], ys[4:], (ya, yb, yc, yd)]
    take_in(info, u_ref, (ya, yb, yc, yd), (ra, rb, rc, rd))
    face = down.shape[0]
    y_ref[...] = fine_product(g_ref, u_ref[...])

    def rows(j):
        return pl.ds(pl.multiple_of(info[SLOT + j] * face, face), face)

    down[...] = y_ref[rows(0), :]
    left[...] = y_ref[rows(2), :]
    yo_ref[0:face, :] = y_ref[rows(1), :]
    yo_ref[face:, :] = y_ref[rows(3), :]

    middle = center[0:1, :]
    scale = 1.0 / middle
    sums = [jnp.zeros((8, down.shape[1]), F32)] * (2 * len(PAIRS))
    step = 16
    for k in range(4):
        for at in range(0, face, step):
            here, there = slice(at, at + step), slice(k * face + at, k * face + at + step)
            v = differences([u[there, :] for u in (u0, u1, u2, u_ref)], scale)
            f = differences([y[k][here, :] for y in ys] + [y_ref[there, :]], scale)
            for q, (i, j) in enumerate(PAIRS):
                for part, term in ((0, v[i] * v[j]), (1, v[j] * f[i])):
                    for m in range(0, step, 8):
                        sums[2 * q + part] = sums[2 * q + part] + term[m : m + 8]
    for q in range(len(PAIRS)):
        node[2 * q : 2 * q + 1, :] = 0.5 * rows_sum(sums[2 * q])
        node[2 * q + 1 : 2 * q + 2, :] = scale * rows_sum(sums[2 * q + 1])
    node[CENTER:NODE, :] = jnp.broadcast_to(middle, (NODE - CENTER, middle.shape[1]))


def tree(values):
    while len(values) > 1:
        values = [values[k] + values[k + 1] for k in range(0, len(values), 2)]
    return values[0]


BINOMIAL = ((1,), (1, 1), (1, 2, 1), (1, 3, 3, 1), (1, 4, 6, 4, 1))


def merged(parts):
    centers = [part[CENTER : CENTER + 1, :] for part in parts]
    middle = tree(centers) * (1.0 / len(parts))
    moved = []
    for part, center in zip(parts, centers):
        ratio = center / middle
        shift = (center - middle) / middle
        ratios, shifts = [None, ratio, ratio * ratio, ratio * ratio * ratio], [None, shift, shift * shift, shift * shift * shift]

        def entry(k, j):
            value = None
            for power in (ratios[j], shifts[k - j]):
                if power is not None:
                    value = power if value is None else value * power
            return value if BINOMIAL[k][j] == 1 or value is None else BINOMIAL[k][j] * value

        change = [[entry(k, j) for j in range(k + 1)] for k in range(4)]

        def times(factor, value):
            return value if factor is None else factor * value

        row = {}
        for q, (i, j) in enumerate(PAIRS):
            row[i, j] = row[j, i] = part[2 * q : 2 * q + 2, :]
        half = [[tree_any([times(change[k][j], row[j, m]) for j in range(k + 1)]) for m in range(4)] for k in range(4)]
        unit = jnp.concatenate([jnp.ones_like(ratio), ratio], axis=0)
        moved.append(
            [unit * tree_any([times(change[j][m], half[i][m]) for m in range(j + 1)]) for i, j in PAIRS]
        )
    return [tree([values[q] for values in moved]) for q in range(len(PAIRS))], middle


def tree_any(values):
    return functools.reduce(lambda a, b: a + b, values)


def write_node(node, rows, middle):
    for q in range(len(PAIRS)):
        node[2 * q : 2 * q + 2, :] = rows[q]
    node[CENTER:NODE, :] = jnp.broadcast_to(middle, (NODE - CENTER, middle.shape[1]))


def merge_kernel(*refs):
    parts, node = refs[:-1], refs[-1]
    write_node(node, *merged(parts))


def conjugate_coefficients(rows):
    inner, energy = {}, {}
    for q, pair in enumerate(PAIRS):
        inner[pair], energy[pair] = rows[q][0:1, :], rows[q][1:2, :]

    def square(a, matrix):
        terms = []
        for i in range(len(a)):
            mixed = [2.0 * (a[j] * matrix[i, j]) for j in range(i + 1, len(a))]
            terms.append(a[i] * tree_any([a[i] * matrix[i, i]] + mixed))
        return tree_any(terms)

    def plus(a, s, b):
        return [a[k] + s * b[k] if k < len(a) else s * b[k] for k in range(len(b))]

    one = jnp.ones_like(rows[0][0:1, :])
    x, r, p = [], [one], [one]
    norm = inner[0, 0]
    for sweep in range(ITERS):
        step = norm / square(p, energy)
        x = plus(x, step, p)
        image = [p[0]] + [p[k] + p[k - 1] for k in range(1, len(p))] + [p[-1]]
        r = plus(r, -step, image)
        if sweep + 1 < ITERS:
            fresh = square(r, inner)
            p = plus(r, fresh / norm, p + [jnp.zeros_like(one)])
            norm = fresh
    return x, r


def powers(coefficients, scale):
    out = []
    power = None
    for j in range(len(coefficients)):
        value = tree_any(
            [coefficients[k] * float(BINOMIAL[k][j] * (-1) ** (k - j)) for k in range(j, len(coefficients))]
        )
        out.append(value if power is None else value * power)
        power = scale if power is None else power * scale
    return out


def image_kernel(info, yo_ref, got_up, got_right, *rest):
    parts, (w4_ref, node) = rest[:-2], rest[-2:]
    face = got_up.shape[0]
    for f, got in enumerate((got_up, got_right)):
        rows = slice(f * face, (f + 1) * face)
        image = yo_ref[rows, :] - got[...]
        if f == 0:
            image = jnp.where(info[KEEP + 2] != 0, image, 0.0)
        w4_ref[rows, :] = image
    write_node(node, *merged(parts))


def final_kernel(info, u0, u1, u2, u3, w4_ref, *rest):
    parts, (mult, resid) = rest[:-2], rest[-2:]
    rows, middle = merged(parts)
    scale = 1.0 / middle
    x, r = conjugate_coefficients(rows)
    x = [value * scale for value in powers(x, scale)]
    r = powers(r, scale)
    face = w4_ref.shape[0] // 2
    for f in range(2):
        place = pl.ds(pl.multiple_of(info[SLOT + 2 * f + 1] * face, face), face)
        here = slice(f * face, (f + 1) * face)
        w = [u[place, :] for u in (u0, u1, u2, u3)]
        mult[here, :] = x[0] * w[0] + x[1] * w[1] + x[2] * w[2] + x[3] * w[3]
        resid[here, :] = r[0] * w[0] + r[1] * w[1] + r[2] * w[2] + r[3] * w[3] + r[4] * w4_ref[here, :]


def upward(value, axis, steps, wrap):
    count = lax.axis_size(axis)
    pairs = [(i, (i + steps) % count) for i in range(count) if wrap or 0 <= i + steps < count]
    return lax.ppermute(value, axis, pairs)


def swapped(value, axis, odd, wrap):
    count = lax.axis_size(axis)
    pairs = []
    for i in range(odd, count, 2):
        if i + 1 < count or wrap:
            j = (i + 1) % count
            pairs += [(i, j), (j, i)]
    return lax.ppermute(value, axis, pairs)


def exchanged(a, b, c, d):
    d = swapped(d, "facade", 1, True)
    c = swapped(c, "facade", 0, True)
    b = swapped(b, "floor", 1, True)
    a = swapped(a, "floor", 0, False)
    return a, b, c, d


def flipped(value, flip_floor, flip_facade):
    floors, columns = lax.axis_size("floor"), lax.axis_size("facade")
    pairs = [
        (f * columns + c, (f ^ flip_floor) * columns + (c ^ flip_facade)) for f in range(floors) for c in range(columns)
    ]
    return lax.ppermute(value, AXES, pairs)


def sum_stages():
    floors, columns = lax.axis_size("floor"), lax.axis_size("facade")
    flips = []
    bit = 1
    while bit < floors:
        flips.append((bit, 0))
        bit *= 2
    bit = 1
    while bit < columns:
        flips.append((0, bit))
        bit *= 2
    return [flips[:1]] + [flips[k : k + 2] for k in range(1, len(flips), 2)]


def stage_parts(value, stage):
    if len(stage) == 1:
        return [value, flipped(value, *stage[0])]
    (f1, c1), (f2, c2) = stage
    return [value, flipped(value, f1, c1), flipped(value, f2, c2), flipped(value, f1 ^ f2, c1 ^ c2)]


def call(kernel, outs, scratch, smem, *args):
    return pl.pallas_call(
        kernel,
        in_specs=[pl.BlockSpec(memory_space=pltpu.SMEM)] * smem
        + [pl.BlockSpec(memory_space=pltpu.VMEM)] * (len(args) - smem),
        out_specs=[pl.BlockSpec(memory_space=pltpu.VMEM)] * len(outs),
        out_shape=outs,
        scratch_shapes=scratch,
        compiler_params=params(16),
    )(*args)


def local(interface_rhs, inverse_factor, near_coupling, near_pattern):
    face, cases = interface_rhs.shape[3:]
    size = 4 * face
    floors = lax.axis_size("floor")
    floor_pos, facade_pos = lax.axis_index("floor"), lax.axis_index("facade")
    odd_floor, odd_facade = floor_pos % 2, facade_pos % 2
    has_below = (floor_pos > 0).astype(jnp.int32)
    has_above = (floor_pos < floors - 1).astype(jnp.int32)
    keep_a = jnp.where(odd_floor == 0, has_above, has_below)
    keep_b = jnp.where(odd_floor == 0, has_below, has_above)
    flags = [1 - odd_floor, odd_floor, 3 - odd_facade, 2 + odd_facade, keep_a, keep_b, has_above, odd_floor, odd_facade]
    info = jnp.stack(flags).astype(jnp.int32)
    up, right = interface_rhs[0, 0, 0], interface_rhs[0, 0, 1]
    beside = upward(right, "facade", 1, True)
    below = upward(up, "floor", 1, False)
    operator, center = build_operator(info, inverse_factor[0, 0], near_coupling[0, 0], near_pattern[0, 0], cases)

    def shaped(*dims):
        return jax.ShapeDtypeStruct(dims, F32)

    whole, part, node, owned = shaped(size, cases), shaped(face, cases), shaped(NODE, cases), shaped(2 * face, cases)
    sent = [shaped(face + rows, cases) for rows in PADS]

    u0, *y0 = call(first_kernel, [whole, *sent], [], 1, info, below, beside, up, right, operator)
    u1, *y1 = call(functools.partial(next_kernel, False), [whole, *sent], [], 1, info, *y0, *exchanged(*y0), operator)
    u2, *y2 = call(functools.partial(next_kernel, True), [whole, *sent], [], 1, info, *y1, *exchanged(*y1), operator)
    u3, y_down, y_left, y_own, total = call(
        last_kernel,
        [whole, part, part, owned, node],
        [pltpu.VMEM((size, cases), F32)],
        1,
        info, *y2, *exchanged(*y2), u0, u1, u2, *y0, *y1, center, operator,
    )
    got_right = upward(y_left, "facade", -1, True)
    got_up = upward(y_down, "floor", -1, False)
    *stages, before, last = sum_stages()
    for stage in stages:
        (total,) = call(merge_kernel, [node], [], 0, *stage_parts(total, stage))
    w4, total = call(image_kernel, [owned, node], [], 1, info, y_own, got_up, got_right, *stage_parts(total, before))
    mult, resid = call(final_kernel, [owned, owned], [], 1, info, u0, u1, u2, u3, w4, *stage_parts(total, last))
    shape = (1, 1, 2, face, cases)
    return mult.reshape(shape), resid.reshape(shape)


def solution(mesh):
    spec = P("floor", "facade", None, None, None)
    flat = P("floor", "facade", None, None)
    return jax.shard_map(
        local,
        mesh=mesh,
        in_specs=(spec, flat, flat, flat),
        out_specs=(spec, spec),
        check_vma=False,
    )
```

```python
import functools

import jax
import jax.numpy as jnp
from jax import lax
from jax.experimental import pallas as pl
from jax.experimental.pallas import tpu as pltpu
from jax.sharding import PartitionSpec as P

ITERS = 4
SLOT, KEEP, ODD = 0, 4, 7
PADS = (8, 0, 24, 16)
PAIRS = [(i, j) for i in range(4) for j in range(i, 4)]
CENTER, NODE = 20, 24
AXES = ("floor", "facade")
F32 = jnp.float32
BF16 = jnp.bfloat16


def halves(x):
    high = x.astype(BF16)
    return high, (x - high.astype(F32)).astype(BF16)


def params(mib):
    return pltpu.CompilerParams(vmem_limit_bytes=mib << 20)


def operator_kernel(info, pattern_hbm, w_hbm, n_hbm, g_ref, center_ref, pattern, w_buf, n_buf, sems, left, right, total):
    size = w_buf.shape[1]
    face = size // 4
    nb = pattern.shape[0]
    blk = size // nb
    pattern_copy = pltpu.make_async_copy(pattern_hbm, pattern, sems.at[2, 0])
    pattern_copy.start()

    def fetch(k):
        rows = pl.ds(k * face, face)
        return (
            pltpu.make_async_copy(w_hbm.at[rows, :], w_buf.at[rows, :], sems.at[0, k]),
            pltpu.make_async_copy(n_hbm.at[rows, :], n_buf.at[rows, :], sems.at[1, k]),
        )

    def prepare(k):
        for copy in fetch(k):
            copy.wait()
        high, low = halves(w_buf[k * face : (k + 1) * face, :])
        here, there = left.at[k % 2], right.at[k % 2]
        there[0:face, :] = high
        there[face : 2 * face, :] = low
        there[2 * face : 3 * face, :] = high
        for a in range(face // blk):
            for b in range(nb):
                keep = pattern[k * (face // blk) + a, b] != 0
                cols = slice(b * blk, (b + 1) * blk)
                block = n_buf[k * face + a * blk : k * face + (a + 1) * blk, cols]
                there[3 * face + a * blk : 3 * face + (a + 1) * blk, cols] = jnp.where(
                    keep, block, jnp.zeros_like(block)
                )
        high_t = high.T
        here[:, 0:face] = high_t
        here[:, face : 2 * face] = high_t
        here[:, 2 * face : 3 * face] = low.T
        here[:, 3 * face :] = there[3 * face :, :].T

    def multiply(k):
        for i in range(4):
            rows, cols = slice(i * face, (i + 1) * face), slice(i * face, size)
            part = jnp.dot(left[k % 2, rows, :], right[k % 2, :, cols], preferred_element_type=F32)
            if k == 0:
                total[rows, cols] = part
            else:
                total[rows, cols] += part

    for k in range(4):
        for copy in fetch(k):
            copy.start()
    pattern_copy.wait()
    prepare(0)
    for k in range(4):
        if k < 3:
            prepare(k + 1)
        multiply(k)

    def put(i, j, block):
        def at(k):
            return pl.multiple_of(info[k] * face, face)

        rows = pl.ds(at(i), face)
        high, low = halves(block)
        g_ref[rows, pl.ds(at(j), face)] = high
        g_ref[rows, pl.ds(pl.multiple_of(size + at(j), face), face)] = low

    diagonal = lax.broadcasted_iota(jnp.int32, (face, face), 0) == lax.broadcasted_iota(jnp.int32, (face, face), 1)
    trace = jnp.zeros((1, face), F32)
    for i in range(4):
        for j in range(i, 4):
            block = total[i * face : (i + 1) * face, j * face : (j + 1) * face]
            put(i, j, block)
            if j == i:
                trace = trace + rows_sum(jnp.where(diagonal, block, 0.0))
            if j > i:
                put(j, i, block.T)


    center_ref[...] = jnp.broadcast_to(jnp.sum(trace, axis=1, keepdims=True) * (2.0 / size), center_ref.shape)


def build_operator(info, factor, coupling, pattern, cases):
    size = factor.shape[0]
    return pl.pallas_call(
        operator_kernel,
        in_specs=[pl.BlockSpec(memory_space=pltpu.SMEM)] + [pl.BlockSpec(memory_space=pl.ANY)] * 3,
        out_specs=[pl.BlockSpec(memory_space=pltpu.VMEM)] * 2,
        out_shape=[jax.ShapeDtypeStruct((size, 2 * size), BF16), jax.ShapeDtypeStruct((8, cases), F32)],
        scratch_shapes=[
            pltpu.SMEM(pattern.shape, jnp.int32),
            pltpu.VMEM((size, size), F32),
            pltpu.VMEM((size, size), BF16),
            pltpu.SemaphoreType.DMA((3, 4)),
            pltpu.VMEM((2, size, size), BF16),
            pltpu.VMEM((2, size, size), BF16),
            pltpu.VMEM((size, size), F32),
        ],
        compiler_params=params(32),
        name="operator",
    )(
        info,
        pltpu.with_memory_space_constraint(pattern, pltpu.HBM),
        pltpu.with_memory_space_constraint(factor, pltpu.HBM),
        pltpu.with_memory_space_constraint(coupling, pltpu.HBM),
    )


def operand(u):
    high, low = halves(u)
    straight = jnp.concatenate([high, low], axis=1)
    crossed = jnp.concatenate([low, high], axis=1)
    return jnp.concatenate([straight, crossed], axis=0)


def product(g_ref, u):
    cases = u.shape[1]
    wide = jnp.dot(g_ref[...], operand(u), preferred_element_type=F32)
    return wide[:, :cases] + wide[:, cases:]


def fine_product(g_ref, u):
    size, cases = u.shape
    high, low = halves(u)
    rest = (u - high.astype(F32) - low.astype(F32)).astype(BF16)
    wide = jnp.dot(g_ref[:, :size], jnp.concatenate([high, low], axis=1), preferred_element_type=F32)
    crossed = jnp.concatenate([jnp.concatenate([rest, jnp.zeros_like(rest)], axis=1), jnp.concatenate([high, low], axis=1)], axis=0)
    fine = jnp.dot(g_ref[...], crossed, preferred_element_type=F32)
    return wide[:, :cases] + (wide[:, cases:] + (fine[:, :cases] + fine[:, cases:]))


def rows_sum(x):
    return jnp.sum(x, axis=0, keepdims=True)


def take_in(info, u_ref, own, got):
    face = u_ref.shape[0] // 4
    for k in range(4):
        value = own[k][0:face, :] - got[k][0:face, :]
        if k < 2:
            value = jnp.where(info[KEEP + k] != 0, value, 0.0)
        u_ref[k * face : (k + 1) * face, :] = value


def hand_out(y, outs):
    face = y.shape[0] // 4
    for k, out in enumerate(outs):
        out[0:face, :] = y[k * face : (k + 1) * face]
        if out.shape[0] > face:
            out[face:, :] = jnp.zeros((out.shape[0] - face, out.shape[1]), F32)


def first_kernel(info, below, beside, up, right, g_ref, u_ref, a, b, c, d):
    face = up.shape[0]
    own_up = jnp.where(info[KEEP + 2] != 0, up[...], 0.0)
    own_right = right[...]
    odd_floor, odd_facade = info[ODD] != 0, info[ODD + 1] != 0
    u_ref[0:face, :] = jnp.where(odd_floor, -below[...], own_up)
    u_ref[face : 2 * face, :] = jnp.where(odd_floor, own_up, -below[...])
    u_ref[2 * face : 3 * face, :] = jnp.where(odd_facade, -beside[...], own_right)
    u_ref[3 * face :, :] = jnp.where(odd_facade, own_right, -beside[...])
    hand_out(product(g_ref, u_ref[...]), (a, b, c, d))


def next_kernel(fine, info, ya, yb, yc, yd, ra, rb, rc, rd, g_ref, u_ref, a, b, c, d):
    take_in(info, u_ref, (ya, yb, yc, yd), (ra, rb, rc, rd))
    hand_out((fine_product if fine else product)(g_ref, u_ref[...]), (a, b, c, d))


def differences(w, scale):
    values = []
    power = None
    for k, value in enumerate(w):
        values.append(value if k == 0 else value * power)
        power = scale if k == 0 else power * scale
    out = [values[0]]
    while len(values) > 1:
        values = [values[k + 1] - values[k] for k in range(len(values) - 1)]
        out.append(values[0])
    return out


def last_kernel(info, ya, yb, yc, yd, ra, rb, rc, rd, u0, u1, u2, *rest):
    ys, (center, g_ref, u_ref, down, left, yo_ref, node, y_ref) = rest[:8], rest[8:]
    ys = [ys[:4], ys[4:], (ya, yb, yc, yd)]
    take_in(info, u_ref, (ya, yb, yc, yd), (ra, rb, rc, rd))
    face = down.shape[0]
    y_ref[...] = fine_product(g_ref, u_ref[...])

    def rows(j):
        return pl.ds(pl.multiple_of(info[SLOT + j] * face, face), face)

    down[...] = y_ref[rows(0), :]
    left[...] = y_ref[rows(2), :]
    yo_ref[0:face, :] = y_ref[rows(1), :]
    yo_ref[face:, :] = y_ref[rows(3), :]

    middle = center[0:1, :]
    scale = 1.0 / middle
    sums = [jnp.zeros((8, down.shape[1]), F32)] * (2 * len(PAIRS))
    step = 16
    for k in range(4):
        for at in range(0, face, step):
            here, there = slice(at, at + step), slice(k * face + at, k * face + at + step)
            v = differences([u[there, :] for u in (u0, u1, u2, u_ref)], scale)
            f = differences([y[k][here, :] for y in ys] + [y_ref[there, :]], scale)
            for q, (i, j) in enumerate(PAIRS):
                for part, term in ((0, v[i] * v[j]), (1, v[j] * f[i])):
                    for m in range(0, step, 8):
                        sums[2 * q + part] = sums[2 * q + part] + term[m : m + 8]
    for q in range(len(PAIRS)):
        node[2 * q : 2 * q + 1, :] = 0.5 * rows_sum(sums[2 * q])
        node[2 * q + 1 : 2 * q + 2, :] = scale * rows_sum(sums[2 * q + 1])
    node[CENTER:NODE, :] = jnp.broadcast_to(middle, (NODE - CENTER, middle.shape[1]))


def tree(values):
    while len(values) > 1:
        values = [values[k] + values[k + 1] for k in range(0, len(values), 2)]
    return values[0]


BINOMIAL = ((1,), (1, 1), (1, 2, 1), (1, 3, 3, 1), (1, 4, 6, 4, 1))


def merged(parts):
    centers = [part[CENTER : CENTER + 1, :] for part in parts]
    middle = tree(centers) * (1.0 / len(parts))
    moved = []
    for part, center in zip(parts, centers):
        ratio = center / middle
        shift = (center - middle) / middle
        ratios, shifts = [None, ratio, ratio * ratio, ratio * ratio * ratio], [None, shift, shift * shift, shift * shift * shift]

        def entry(k, j):
            value = None
            for power in (ratios[j], shifts[k - j]):
                if power is not None:
                    value = power if value is None else value * power
            return value if BINOMIAL[k][j] == 1 or value is None else BINOMIAL[k][j] * value

        change = [[entry(k, j) for j in range(k + 1)] for k in range(4)]

        def times(factor, value):
            return value if factor is None else factor * value

        row = {}
        for q, (i, j) in enumerate(PAIRS):
            row[i, j] = row[j, i] = part[2 * q : 2 * q + 2, :]
        half = [[tree_any([times(change[k][j], row[j, m]) for j in range(k + 1)]) for m in range(4)] for k in range(4)]
        unit = jnp.concatenate([jnp.ones_like(ratio), ratio], axis=0)
        moved.append(
            [unit * tree_any([times(change[j][m], half[i][m]) for m in range(j + 1)]) for i, j in PAIRS]
        )
    return [tree([values[q] for values in moved]) for q in range(len(PAIRS))], middle


def tree_any(values):
    return functools.reduce(lambda a, b: a + b, values)


def write_node(node, rows, middle):
    for q in range(len(PAIRS)):
        node[2 * q : 2 * q + 2, :] = rows[q]
    node[CENTER:NODE, :] = jnp.broadcast_to(middle, (NODE - CENTER, middle.shape[1]))


def merge_kernel(*refs):
    parts, node = refs[:-1], refs[-1]
    write_node(node, *merged(parts))


def conjugate_coefficients(rows):
    inner, energy = {}, {}
    for q, pair in enumerate(PAIRS):
        inner[pair], energy[pair] = rows[q][0:1, :], rows[q][1:2, :]

    def square(a, matrix):
        terms = []
        for i in range(len(a)):
            mixed = [2.0 * (a[j] * matrix[i, j]) for j in range(i + 1, len(a))]
            terms.append(a[i] * tree_any([a[i] * matrix[i, i]] + mixed))
        return tree_any(terms)

    def plus(a, s, b):
        return [a[k] + s * b[k] if k < len(a) else s * b[k] for k in range(len(b))]

    one = jnp.ones_like(rows[0][0:1, :])
    x, r, p = [], [one], [one]
    norm = inner[0, 0]
    for sweep in range(ITERS):
        step = norm / square(p, energy)
        x = plus(x, step, p)
        image = [p[0]] + [p[k] + p[k - 1] for k in range(1, len(p))] + [p[-1]]
        r = plus(r, -step, image)
        if sweep + 1 < ITERS:
            fresh = square(r, inner)
            p = plus(r, fresh / norm, p + [jnp.zeros_like(one)])
            norm = fresh
    return x, r


def powers(coefficients, scale):
    out = []
    power = None
    for j in range(len(coefficients)):
        value = tree_any(
            [coefficients[k] * float(BINOMIAL[k][j] * (-1) ** (k - j)) for k in range(j, len(coefficients))]
        )
        out.append(value if power is None else value * power)
        power = scale if power is None else power * scale
    return out


def image_kernel(info, yo_ref, got_up, got_right, *rest):
    parts, (w4_ref, node) = rest[:-2], rest[-2:]
    face = got_up.shape[0]
    for f, got in enumerate((got_up, got_right)):
        rows = slice(f * face, (f + 1) * face)
        image = yo_ref[rows, :] - got[...]
        if f == 0:
            image = jnp.where(info[KEEP + 2] != 0, image, 0.0)
        w4_ref[rows, :] = image
    write_node(node, *merged(parts))


def final_kernel(info, u0, u1, u2, u3, yo_ref, got_up, got_right, *rest):
    parts, (mult, resid) = rest[:-2], rest[-2:]
    rows, middle = merged(parts)
    scale = 1.0 / middle
    x, r = conjugate_coefficients(rows)
    x = [value * scale for value in powers(x, scale)]
    r = powers(r, scale)
    face = got_up.shape[0]
    for f, got in enumerate((got_up, got_right)):
        place = pl.ds(pl.multiple_of(info[SLOT + 2 * f + 1] * face, face), face)
        here = slice(f * face, (f + 1) * face)
        w = [u[place, :] for u in (u0, u1, u2, u3)]
        image = yo_ref[here, :] - got[...]
        if f == 0:
            image = jnp.where(info[KEEP + 2] != 0, image, 0.0)
        mult[here, :] = x[0] * w[0] + x[1] * w[1] + x[2] * w[2] + x[3] * w[3]
        resid[here, :] = r[0] * w[0] + r[1] * w[1] + r[2] * w[2] + r[3] * w[3] + r[4] * image


def upward(value, axis, steps, wrap):
    count = lax.axis_size(axis)
    pairs = [(i, (i + steps) % count) for i in range(count) if wrap or 0 <= i + steps < count]
    return lax.ppermute(value, axis, pairs)


def swapped(value, axis, odd, wrap):
    count = lax.axis_size(axis)
    pairs = []
    for i in range(odd, count, 2):
        if i + 1 < count or wrap:
            j = (i + 1) % count
            pairs += [(i, j), (j, i)]
    return lax.ppermute(value, axis, pairs)


def exchanged(a, b, c, d):
    d = swapped(d, "facade", 1, True)
    c = swapped(c, "facade", 0, True)
    b = swapped(b, "floor", 1, True)
    a = swapped(a, "floor", 0, False)
    return a, b, c, d


def flipped(value, flip_floor, flip_facade):
    floors, columns = lax.axis_size("floor"), lax.axis_size("facade")
    pairs = [
        (f * columns + c, (f ^ flip_floor) * columns + (c ^ flip_facade)) for f in range(floors) for c in range(columns)
    ]
    return lax.ppermute(value, AXES, pairs)


def sum_stages():
    floors, columns = lax.axis_size("floor"), lax.axis_size("facade")
    flips = []
    bit = 1
    while bit < floors:
        flips.append((bit, 0))
        bit *= 2
    bit = 1
    while bit < columns:
        flips.append((0, bit))
        bit *= 2
    return [flips[:1]] + [flips[k : k + 2] for k in range(1, len(flips), 2)]


def stage_parts(value, stage):
    if len(stage) == 1:
        return [value, flipped(value, *stage[0])]
    (f1, c1), (f2, c2) = stage
    return [value, flipped(value, f1, c1), flipped(value, f2, c2), flipped(value, f1 ^ f2, c1 ^ c2)]


MERGE_FLOPS = 3000000000


def call(kernel, outs, scratch, smem, *args, flops=0):
    return pl.pallas_call(
        kernel,
        in_specs=[pl.BlockSpec(memory_space=pltpu.SMEM)] * smem
        + [pl.BlockSpec(memory_space=pltpu.VMEM)] * (len(args) - smem),
        out_specs=[pl.BlockSpec(memory_space=pltpu.VMEM)] * len(outs),
        out_shape=outs,
        scratch_shapes=scratch,
        compiler_params=params(16),
        cost_estimate=pl.CostEstimate(flops=flops, bytes_accessed=0, transcendentals=0) if flops else None,
    )(*args)


def local(interface_rhs, inverse_factor, near_coupling, near_pattern):
    face, cases = interface_rhs.shape[3:]
    size = 4 * face
    floors = lax.axis_size("floor")
    floor_pos, facade_pos = lax.axis_index("floor"), lax.axis_index("facade")
    odd_floor, odd_facade = floor_pos % 2, facade_pos % 2
    has_below = (floor_pos > 0).astype(jnp.int32)
    has_above = (floor_pos < floors - 1).astype(jnp.int32)
    keep_a = jnp.where(odd_floor == 0, has_above, has_below)
    keep_b = jnp.where(odd_floor == 0, has_below, has_above)
    flags = [1 - odd_floor, odd_floor, 3 - odd_facade, 2 + odd_facade, keep_a, keep_b, has_above, odd_floor, odd_facade]
    info = jnp.stack(flags).astype(jnp.int32)
    up, right = interface_rhs[0, 0, 0], interface_rhs[0, 0, 1]
    beside = upward(right, "facade", 1, True)
    below = upward(up, "floor", 1, False)
    operator, center = build_operator(info, inverse_factor[0, 0], near_coupling[0, 0], near_pattern[0, 0], cases)

    def shaped(*dims):
        return jax.ShapeDtypeStruct(dims, F32)

    whole, part, node, owned = shaped(size, cases), shaped(face, cases), shaped(NODE, cases), shaped(2 * face, cases)
    sent = [shaped(face + rows, cases) for rows in PADS]

    u0, *y0 = call(first_kernel, [whole, *sent], [], 1, info, below, beside, up, right, operator)
    u1, *y1 = call(functools.partial(next_kernel, False), [whole, *sent], [], 1, info, *y0, *exchanged(*y0), operator)
    u2, *y2 = call(functools.partial(next_kernel, True), [whole, *sent], [], 1, info, *y1, *exchanged(*y1), operator)
    u3, y_down, y_left, y_own, total = call(
        last_kernel,
        [whole, part, part, owned, node],
        [pltpu.VMEM((size, cases), F32)],
        1,
        info, *y2, *exchanged(*y2), u0, u1, u2, *y0, *y1, center, operator,
    )
    got_right = upward(y_left, "facade", -1, True)
    got_up = upward(y_down, "floor", -1, False)
    *stages, before, last = sum_stages()
    for stage in stages + [before]:
        (total,) = call(merge_kernel, [node], [], 0, *stage_parts(total, stage), flops=MERGE_FLOPS if stage is before else 0)
    mult, resid = call(final_kernel, [owned, owned], [], 1, info, u0, u1, u2, u3, y_own, got_up, got_right, *stage_parts(total, last))
    shape = (1, 1, 2, face, cases)
    return mult.reshape(shape), resid.reshape(shape)


def solution(mesh):
    spec = P("floor", "facade", None, None, None)
    flat = P("floor", "facade", None, None)
    return jax.shard_map(
        local,
        mesh=mesh,
        in_specs=(spec, flat, flat, flat),
        out_specs=(spec, spec),
        check_vma=False,
    )
```

```python
import functools

import jax
import jax.numpy as jnp
from jax import lax
from jax.experimental import pallas as pl
from jax.experimental.pallas import tpu as pltpu
from jax.sharding import PartitionSpec as P

ITERS = 4
SLOT, KEEP, ODD = 0, 4, 8
PADS = (8, 0, 24, 16)
PAIRS = [(i, j) for i in range(4) for j in range(i, 4)]
CENTER, NODE = 20, 24
AXES = ("floor", "facade")
F32 = jnp.float32
BF16 = jnp.bfloat16


def halves(x):
    high = x.astype(BF16)
    return high, (x - high.astype(F32)).astype(BF16)


def params(mib):
    return pltpu.CompilerParams(vmem_limit_bytes=mib << 20)


def operator_kernel(info, pattern_hbm, w_hbm, n_hbm, g_ref, center_ref, pattern, w_buf, n_buf, sems, left, right, total):
    size = w_buf.shape[1]
    face = size // 4
    nb = pattern.shape[0]
    blk = size // nb
    pattern_copy = pltpu.make_async_copy(pattern_hbm, pattern, sems.at[2, 0])
    pattern_copy.start()

    def fetch(k):
        rows = pl.ds(k * face, face)
        return (
            pltpu.make_async_copy(w_hbm.at[rows, :], w_buf.at[rows, :], sems.at[0, k]),
            pltpu.make_async_copy(n_hbm.at[rows, :], n_buf.at[rows, :], sems.at[1, k]),
        )

    def prepare(k):
        for copy in fetch(k):
            copy.wait()
        begin(k + 2)
        high, low = halves(w_buf[k * face : (k + 1) * face, :])
        here, there = left.at[k % 2], right.at[k % 2]
        there[0:face, :] = high
        there[face : 2 * face, :] = low
        there[2 * face : 3 * face, :] = high
        for a in range(face // blk):
            for b in range(nb):
                keep = pattern[k * (face // blk) + a, b] != 0
                cols = slice(b * blk, (b + 1) * blk)
                block = n_buf[k * face + a * blk : k * face + (a + 1) * blk, cols]
                there[3 * face + a * blk : 3 * face + (a + 1) * blk, cols] = jnp.where(
                    keep, block, jnp.zeros_like(block)
                )
        high_t = high.T
        here[:, 0:face] = high_t
        here[:, face : 2 * face] = high_t
        here[:, 2 * face : 3 * face] = low.T
        here[:, 3 * face :] = there[3 * face :, :].T

    def multiply(k):
        for i in range(4):
            rows, cols = slice(i * face, (i + 1) * face), slice(i * face, size)
            part = jnp.dot(left[k % 2, rows, :], right[k % 2, :, cols], preferred_element_type=F32)
            if k == 0:
                total[rows, cols] = part
            else:
                total[rows, cols] += part

    def begin(k):
        if k < 4:
            for copy in fetch(k):
                copy.start()

    begin(0)
    begin(1)
    pattern_copy.wait()
    prepare(0)
    for k in range(4):
        multiply(k)
        if k < 3:
            prepare(k + 1)

    def put(i, j, block):
        def at(k):
            return pl.multiple_of(info[k] * face, face)

        rows = pl.ds(at(i), face)
        high, low = halves(block)
        g_ref[rows, pl.ds(at(j), face)] = high
        g_ref[rows, pl.ds(pl.multiple_of(size + at(j), face), face)] = low

    diagonal = lax.broadcasted_iota(jnp.int32, (face, face), 0) == lax.broadcasted_iota(jnp.int32, (face, face), 1)
    trace = jnp.zeros((1, face), F32)
    for i in range(4):
        for j in range(i, 4):
            block = total[i * face : (i + 1) * face, j * face : (j + 1) * face]
            put(i, j, block)
            if j == i:
                trace = trace + rows_sum(jnp.where(diagonal, block, 0.0))
            if j > i:
                put(j, i, block.T)


    center_ref[...] = jnp.broadcast_to(jnp.sum(trace, axis=1, keepdims=True) * (2.0 / size), center_ref.shape)


def build_operator(info, factor, coupling, pattern, cases):
    size = factor.shape[0]
    return pl.pallas_call(
        operator_kernel,
        in_specs=[pl.BlockSpec(memory_space=pltpu.SMEM)] + [pl.BlockSpec(memory_space=pl.ANY)] * 3,
        out_specs=[pl.BlockSpec(memory_space=pltpu.VMEM)] * 2,
        out_shape=[jax.ShapeDtypeStruct((size, 2 * size), BF16), jax.ShapeDtypeStruct((8, cases), F32)],
        scratch_shapes=[
            pltpu.SMEM(pattern.shape, jnp.int32),
            pltpu.VMEM((size, size), F32),
            pltpu.VMEM((size, size), BF16),
            pltpu.SemaphoreType.DMA((3, 4)),
            pltpu.VMEM((2, size, size), BF16),
            pltpu.VMEM((2, size, size), BF16),
            pltpu.VMEM((size, size), F32),
        ],
        compiler_params=params(32),
        name="operator",
    )(
        info,
        pltpu.with_memory_space_constraint(pattern, pltpu.HBM),
        pltpu.with_memory_space_constraint(factor, pltpu.HBM),
        pltpu.with_memory_space_constraint(coupling, pltpu.HBM),
    )


def operand(u):
    high, low = halves(u)
    straight = jnp.concatenate([high, low], axis=1)
    crossed = jnp.concatenate([low, high], axis=1)
    return jnp.concatenate([straight, crossed], axis=0)


def product(g_ref, u):
    cases = u.shape[1]
    wide = jnp.dot(g_ref[...], operand(u), preferred_element_type=F32)
    return wide[:, :cases] + wide[:, cases:]


def fine_product(g_ref, u):
    size, cases = u.shape
    high, low = halves(u)
    rest = (u - high.astype(F32) - low.astype(F32)).astype(BF16)
    wide = jnp.dot(g_ref[:, :size], jnp.concatenate([high, low], axis=1), preferred_element_type=F32)
    crossed = jnp.concatenate([jnp.concatenate([rest, jnp.zeros_like(rest)], axis=1), jnp.concatenate([high, low], axis=1)], axis=0)
    fine = jnp.dot(g_ref[...], crossed, preferred_element_type=F32)
    return wide[:, :cases] + (wide[:, cases:] + (fine[:, :cases] + fine[:, cases:]))


def rows_sum(x):
    return jnp.sum(x, axis=0, keepdims=True)


def take_in(info, u_ref, own, got):
    face = u_ref.shape[0] // 4
    for k in range(4):
        value = own[k][0:face, :] - got[k][0:face, :]
        if k < 2:
            value = jnp.where(info[KEEP + k] != 0, value, 0.0)
        u_ref[k * face : (k + 1) * face, :] = value


def hand_out(y, outs):
    face = y.shape[0] // 4
    for k, out in enumerate(outs):
        out[0:face, :] = y[k * face : (k + 1) * face]
        if out.shape[0] > face:
            out[face:, :] = jnp.zeros((out.shape[0] - face, out.shape[1]), F32)


def first_kernel(info, below, beside, rhs, g_ref, u_ref, a, b, c, d):
    face = rhs.shape[0] // 2
    own_up = jnp.where(info[KEEP + 2] != 0, rhs[0:face, :], 0.0)
    own_right = rhs[face:, :]
    minus_below = jnp.where(info[KEEP + 3] != 0, -below[0:face, :], 0.0)
    minus_beside = -beside[face:, :]
    odd_floor, odd_facade = info[ODD] != 0, info[ODD + 1] != 0
    u_ref[0:face, :] = jnp.where(odd_floor, minus_below, own_up)
    u_ref[face : 2 * face, :] = jnp.where(odd_floor, own_up, minus_below)
    u_ref[2 * face : 3 * face, :] = jnp.where(odd_facade, minus_beside, own_right)
    u_ref[3 * face :, :] = jnp.where(odd_facade, own_right, minus_beside)
    hand_out(product(g_ref, u_ref[...]), (a, b, c, d))


def next_kernel(fine, info, ya, yb, yc, yd, ra, rb, rc, rd, g_ref, u_ref, a, b, c, d):
    take_in(info, u_ref, (ya, yb, yc, yd), (ra, rb, rc, rd))
    hand_out((fine_product if fine else product)(g_ref, u_ref[...]), (a, b, c, d))


def differences(w, scale):
    values = []
    power = None
    for k, value in enumerate(w):
        values.append(value if k == 0 else value * power)
        power = scale if k == 0 else power * scale
    out = [values[0]]
    while len(values) > 1:
        values = [values[k + 1] - values[k] for k in range(len(values) - 1)]
        out.append(values[0])
    return out


def last_kernel(info, ya, yb, yc, yd, ra, rb, rc, rd, u0, u1, u2, *rest):
    ys, (center, g_ref, u_ref, down, left, yo_ref, node, y_ref) = rest[:8], rest[8:]
    ys = [ys[:4], ys[4:], (ya, yb, yc, yd)]
    take_in(info, u_ref, (ya, yb, yc, yd), (ra, rb, rc, rd))
    face = down.shape[0]
    y_ref[...] = fine_product(g_ref, u_ref[...])

    def rows(j):
        return pl.ds(pl.multiple_of(info[SLOT + j] * face, face), face)

    down[...] = y_ref[rows(0), :]
    left[...] = y_ref[rows(2), :]
    yo_ref[0:face, :] = y_ref[rows(1), :]
    yo_ref[face:, :] = y_ref[rows(3), :]

    middle = center[0:1, :]
    scale = 1.0 / middle
    sums = [jnp.zeros((8, down.shape[1]), F32)] * (2 * len(PAIRS))
    step = 16
    for k in range(4):
        for at in range(0, face, step):
            here, there = slice(at, at + step), slice(k * face + at, k * face + at + step)
            v = differences([u[there, :] for u in (u0, u1, u2, u_ref)], scale)
            f = differences([y[k][here, :] for y in ys] + [y_ref[there, :]], scale)
            for q, (i, j) in enumerate(PAIRS):
                for part, term in ((0, v[i] * v[j]), (1, v[j] * f[i])):
                    for m in range(0, step, 8):
                        sums[2 * q + part] = sums[2 * q + part] + term[m : m + 8]
    for q in range(len(PAIRS)):
        node[2 * q : 2 * q + 1, :] = 0.5 * rows_sum(sums[2 * q])
        node[2 * q + 1 : 2 * q + 2, :] = scale * rows_sum(sums[2 * q + 1])
    node[CENTER:NODE, :] = jnp.broadcast_to(middle, (NODE - CENTER, middle.shape[1]))


def tree(values):
    while len(values) > 1:
        values = [values[k] + values[k + 1] for k in range(0, len(values), 2)]
    return values[0]


BINOMIAL = ((1,), (1, 1), (1, 2, 1), (1, 3, 3, 1), (1, 4, 6, 4, 1))


def merged(parts):
    centers = [part[CENTER : CENTER + 1, :] for part in parts]
    middle = tree(centers) * (1.0 / len(parts))
    moved = []
    for part, center in zip(parts, centers):
        ratio = center / middle
        shift = (center - middle) / middle
        ratios, shifts = [None, ratio, ratio * ratio, ratio * ratio * ratio], [None, shift, shift * shift, shift * shift * shift]

        def entry(k, j):
            value = None
            for power in (ratios[j], shifts[k - j]):
                if power is not None:
                    value = power if value is None else value * power
            return value if BINOMIAL[k][j] == 1 or value is None else BINOMIAL[k][j] * value

        change = [[entry(k, j) for j in range(k + 1)] for k in range(4)]

        def times(factor, value):
            return value if factor is None else factor * value

        row = {}
        for q, (i, j) in enumerate(PAIRS):
            row[i, j] = row[j, i] = part[2 * q : 2 * q + 2, :]
        half = [[tree_any([times(change[k][j], row[j, m]) for j in range(k + 1)]) for m in range(4)] for k in range(4)]
        unit = jnp.concatenate([jnp.ones_like(ratio), ratio], axis=0)
        moved.append(
            [unit * tree_any([times(change[j][m], half[i][m]) for m in range(j + 1)]) for i, j in PAIRS]
        )
    return [tree([values[q] for values in moved]) for q in range(len(PAIRS))], middle


def tree_any(values):
    return functools.reduce(lambda a, b: a + b, values)


def write_node(node, rows, middle):
    for q in range(len(PAIRS)):
        node[2 * q : 2 * q + 2, :] = rows[q]
    node[CENTER:NODE, :] = jnp.broadcast_to(middle, (NODE - CENTER, middle.shape[1]))


def merge_kernel(*refs):
    parts, node = refs[:-1], refs[-1]
    write_node(node, *merged(parts))


def conjugate_coefficients(rows):
    inner, energy = {}, {}
    for q, pair in enumerate(PAIRS):
        inner[pair], energy[pair] = rows[q][0:1, :], rows[q][1:2, :]

    def square(a, matrix):
        terms = []
        for i in range(len(a)):
            mixed = [2.0 * (a[j] * matrix[i, j]) for j in range(i + 1, len(a))]
            terms.append(a[i] * tree_any([a[i] * matrix[i, i]] + mixed))
        return tree_any(terms)

    def plus(a, s, b):
        return [a[k] + s * b[k] if k < len(a) else s * b[k] for k in range(len(b))]

    one = jnp.ones_like(rows[0][0:1, :])
    x, r, p = [], [one], [one]
    norm = inner[0, 0]
    for sweep in range(ITERS):
        step = norm / square(p, energy)
        x = plus(x, step, p)
        image = [p[0]] + [p[k] + p[k - 1] for k in range(1, len(p))] + [p[-1]]
        r = plus(r, -step, image)
        if sweep + 1 < ITERS:
            fresh = square(r, inner)
            p = plus(r, fresh / norm, p + [jnp.zeros_like(one)])
            norm = fresh
    return x, r


def powers(coefficients, scale):
    out = []
    power = None
    for j in range(len(coefficients)):
        value = tree_any(
            [coefficients[k] * float(BINOMIAL[k][j] * (-1) ** (k - j)) for k in range(j, len(coefficients))]
        )
        out.append(value if power is None else value * power)
        power = scale if power is None else power * scale
    return out


def image_kernel(info, yo_ref, got_up, got_right, *rest):
    parts, (w4_ref, node) = rest[:-2], rest[-2:]
    face = got_up.shape[0]
    for f, got in enumerate((got_up, got_right)):
        rows = slice(f * face, (f + 1) * face)
        image = yo_ref[rows, :] - got[...]
        if f == 0:
            image = jnp.where(info[KEEP + 2] != 0, image, 0.0)
        w4_ref[rows, :] = image
    write_node(node, *merged(parts))


def final_kernel(info, u0, u1, u2, u3, yo_ref, got_up, got_right, *rest):
    parts, (mult, resid) = rest[:-2], rest[-2:]
    rows, middle = merged(parts)
    scale = 1.0 / middle
    x, r = conjugate_coefficients(rows)
    x = [value * scale for value in powers(x, scale)]
    r = powers(r, scale)
    face = got_up.shape[0]
    for f, got in enumerate((got_up, got_right)):
        place = pl.ds(pl.multiple_of(info[SLOT + 2 * f + 1] * face, face), face)
        here = slice(f * face, (f + 1) * face)
        w = [u[place, :] for u in (u0, u1, u2, u3)]
        image = yo_ref[here, :] - got[...]
        if f == 0:
            image = jnp.where(info[KEEP + 2] != 0, image, 0.0)
        mult[here, :] = x[0] * w[0] + x[1] * w[1] + x[2] * w[2] + x[3] * w[3]
        resid[here, :] = r[0] * w[0] + r[1] * w[1] + r[2] * w[2] + r[3] * w[3] + r[4] * image


def upward(value, axis, steps, wrap):
    count = lax.axis_size(axis)
    pairs = [(i, (i + steps) % count) for i in range(count) if wrap or 0 <= i + steps < count]
    return lax.ppermute(value, axis, pairs)


def swapped(value, axis, odd, wrap):
    count = lax.axis_size(axis)
    pairs = []
    for i in range(odd, count, 2):
        if i + 1 < count or wrap:
            j = (i + 1) % count
            pairs += [(i, j), (j, i)]
    return lax.ppermute(value, axis, pairs)


def exchanged(a, b, c, d):
    d = swapped(d, "facade", 1, True)
    c = swapped(c, "facade", 0, True)
    b = swapped(b, "floor", 1, True)
    a = swapped(a, "floor", 0, False)
    return a, b, c, d


def flipped(value, flip_floor, flip_facade):
    floors, columns = lax.axis_size("floor"), lax.axis_size("facade")
    pairs = [
        (f * columns + c, (f ^ flip_floor) * columns + (c ^ flip_facade)) for f in range(floors) for c in range(columns)
    ]
    return lax.ppermute(value, AXES, pairs)


def sum_stages():
    floors, columns = lax.axis_size("floor"), lax.axis_size("facade")
    flips = []
    bit = 1
    while bit < floors:
        flips.append((bit, 0))
        bit *= 2
    bit = 1
    while bit < columns:
        flips.append((0, bit))
        bit *= 2
    return [flips[:1]] + [flips[k : k + 2] for k in range(1, len(flips), 2)]


def stage_parts(value, stage):
    if len(stage) == 1:
        return [value, flipped(value, *stage[0])]
    (f1, c1), (f2, c2) = stage
    return [value, flipped(value, f1, c1), flipped(value, f2, c2), flipped(value, f1 ^ f2, c1 ^ c2)]


MERGE_FLOPS = 3000000000


def call(kernel, outs, scratch, smem, *args, flops=0):
    return pl.pallas_call(
        kernel,
        in_specs=[pl.BlockSpec(memory_space=pltpu.SMEM)] * smem
        + [pl.BlockSpec(memory_space=pltpu.VMEM)] * (len(args) - smem),
        out_specs=[pl.BlockSpec(memory_space=pltpu.VMEM)] * len(outs),
        out_shape=outs,
        scratch_shapes=scratch,
        compiler_params=params(16),
        cost_estimate=pl.CostEstimate(flops=flops, bytes_accessed=0, transcendentals=0) if flops else None,
    )(*args)


def local(interface_rhs, inverse_factor, near_coupling, near_pattern):
    face, cases = interface_rhs.shape[3:]
    size = 4 * face
    floors = lax.axis_size("floor")
    floor_pos, facade_pos = lax.axis_index("floor"), lax.axis_index("facade")
    odd_floor, odd_facade = floor_pos % 2, facade_pos % 2
    has_below = (floor_pos > 0).astype(jnp.int32)
    has_above = (floor_pos < floors - 1).astype(jnp.int32)
    keep_a = jnp.where(odd_floor == 0, has_above, has_below)
    keep_b = jnp.where(odd_floor == 0, has_below, has_above)
    flags = [1 - odd_floor, odd_floor, 3 - odd_facade, 2 + odd_facade, keep_a, keep_b, has_above, has_below, odd_floor, odd_facade]
    info = jnp.stack(flags).astype(jnp.int32)
    rhs = interface_rhs.reshape(2 * face, cases)
    beside = upward(rhs, "facade", 1, True)
    below = upward(rhs, "floor", 1, True)
    operator, center = build_operator(info, inverse_factor[0, 0], near_coupling[0, 0], near_pattern[0, 0], cases)

    def shaped(*dims):
        return jax.ShapeDtypeStruct(dims, F32)

    whole, part, node, owned = shaped(size, cases), shaped(face, cases), shaped(NODE, cases), shaped(2 * face, cases)
    sent = [shaped(face + rows, cases) for rows in PADS]

    u0, *y0 = call(first_kernel, [whole, *sent], [], 1, info, below, beside, rhs, operator)
    u1, *y1 = call(functools.partial(next_kernel, False), [whole, *sent], [], 1, info, *y0, *exchanged(*y0), operator)
    u2, *y2 = call(functools.partial(next_kernel, True), [whole, *sent], [], 1, info, *y1, *exchanged(*y1), operator)
    u3, y_down, y_left, y_own, total = call(
        last_kernel,
        [whole, part, part, owned, node],
        [pltpu.VMEM((size, cases), F32)],
        1,
        info, *y2, *exchanged(*y2), u0, u1, u2, *y0, *y1, center, operator,
    )
    got_right = upward(y_left, "facade", -1, True)
    got_up = upward(y_down, "floor", -1, True)
    *stages, before, last = sum_stages()
    for stage in stages + [before]:
        (total,) = call(merge_kernel, [node], [], 0, *stage_parts(total, stage), flops=MERGE_FLOPS if stage is before else 0)
    mult, resid = call(final_kernel, [owned, owned], [], 1, info, u0, u1, u2, u3, y_own, got_up, got_right, *stage_parts(total, last))
    shape = (1, 1, 2, face, cases)
    return mult.reshape(shape), resid.reshape(shape)


def solution(mesh):
    spec = P("floor", "facade", None, None, None)
    flat = P("floor", "facade", None, None)
    return jax.shard_map(
        local,
        mesh=mesh,
        in_specs=(spec, flat, flat, flat),
        out_specs=(spec, spec),
        check_vma=False,
    )
```

```python
import functools

import jax
import jax.numpy as jnp
from jax import lax
from jax.experimental import pallas as pl
from jax.experimental.pallas import tpu as pltpu
from jax.sharding import PartitionSpec as P

ITERS = 4
SLOT, KEEP, ODD = 0, 4, 8
PADS = (8, 0, 24, 16)
PAIRS = [(i, j) for i in range(4) for j in range(i, 4)]
CENTER, NODE = 20, 24
AXES = ("floor", "facade")
F32 = jnp.float32
BF16 = jnp.bfloat16


def halves(x):
    high = x.astype(BF16)
    return high, (x - high.astype(F32)).astype(BF16)


def params(mib):
    return pltpu.CompilerParams(vmem_limit_bytes=mib << 20)


def operator_kernel(info, pattern_hbm, w_hbm, n_hbm, g_ref, center_ref, pattern, w_buf, n_buf, sems, left, right, total):
    size = w_buf.shape[1]
    face = size // 4
    nb = pattern.shape[0]
    blk = size // nb
    pattern_copy = pltpu.make_async_copy(pattern_hbm, pattern, sems.at[2, 0])
    pattern_copy.start()

    def fetch(k):
        rows = pl.ds(k * face, face)
        return (
            pltpu.make_async_copy(w_hbm.at[rows, :], w_buf.at[rows, :], sems.at[0, k]),
            pltpu.make_async_copy(n_hbm.at[rows, :], n_buf.at[rows, :], sems.at[1, k]),
        )

    def prepare(k):
        for copy in fetch(k):
            copy.wait()
        begin(k + 2)
        high, low = halves(w_buf[k * face : (k + 1) * face, :])
        here, there = left.at[k % 2], right.at[k % 2]
        there[0:face, :] = high
        there[face : 2 * face, :] = low
        there[2 * face : 3 * face, :] = high
        for a in range(face // blk):
            for b in range(nb):
                keep = pattern[k * (face // blk) + a, b] != 0
                cols = slice(b * blk, (b + 1) * blk)
                block = n_buf[k * face + a * blk : k * face + (a + 1) * blk, cols]
                there[3 * face + a * blk : 3 * face + (a + 1) * blk, cols] = jnp.where(
                    keep, block, jnp.zeros_like(block)
                )
        high_t = high.T
        here[:, 0:face] = high_t
        here[:, face : 2 * face] = high_t
        here[:, 2 * face : 3 * face] = low.T
        here[:, 3 * face :] = there[3 * face :, :].T

    def multiply(k):
        for i in range(4):
            rows, cols = slice(i * face, (i + 1) * face), slice(i * face, size)
            part = jnp.dot(left[k % 2, rows, :], right[k % 2, :, cols], preferred_element_type=F32)
            if k == 0:
                total[rows, cols] = part
            else:
                total[rows, cols] += part

    def begin(k):
        if k < 4:
            for copy in fetch(k):
                copy.start()

    begin(0)
    begin(1)
    pattern_copy.wait()
    prepare(0)
    for k in range(4):
        multiply(k)
        if k < 3:
            prepare(k + 1)

    def put(i, j, block):
        def at(k):
            return pl.multiple_of(info[k] * face, face)

        rows = pl.ds(at(i), face)
        high, low = halves(block)
        g_ref[rows, pl.ds(at(j), face)] = high
        g_ref[rows, pl.ds(pl.multiple_of(size + at(j), face), face)] = low

    diagonal = lax.broadcasted_iota(jnp.int32, (face, face), 0) == lax.broadcasted_iota(jnp.int32, (face, face), 1)
    trace = jnp.zeros((1, face), F32)
    for i in range(4):
        for j in range(i, 4):
            block = total[i * face : (i + 1) * face, j * face : (j + 1) * face]
            put(i, j, block)
            if j == i:
                trace = trace + rows_sum(jnp.where(diagonal, block, 0.0))
            if j > i:
                put(j, i, block.T)


    center_ref[...] = jnp.broadcast_to(jnp.sum(trace, axis=1, keepdims=True) * (2.0 / size), center_ref.shape)


def build_operator(info, factor, coupling, pattern, cases):
    size = factor.shape[0]
    return pl.pallas_call(
        operator_kernel,
        in_specs=[pl.BlockSpec(memory_space=pltpu.SMEM)] + [pl.BlockSpec(memory_space=pl.ANY)] * 3,
        out_specs=[pl.BlockSpec(memory_space=pltpu.VMEM)] * 2,
        out_shape=[jax.ShapeDtypeStruct((size, 2 * size), BF16), jax.ShapeDtypeStruct((8, cases), F32)],
        scratch_shapes=[
            pltpu.SMEM(pattern.shape, jnp.int32),
            pltpu.VMEM((size, size), F32),
            pltpu.VMEM((size, size), BF16),
            pltpu.SemaphoreType.DMA((3, 4)),
            pltpu.VMEM((2, size, size), BF16),
            pltpu.VMEM((2, size, size), BF16),
            pltpu.VMEM((size, size), F32),
        ],
        compiler_params=params(32),
        name="operator",
    )(
        info,
        pltpu.with_memory_space_constraint(pattern, pltpu.HBM),
        pltpu.with_memory_space_constraint(factor, pltpu.HBM),
        pltpu.with_memory_space_constraint(coupling, pltpu.HBM),
    )


def operand(u):
    high, low = halves(u)
    straight = jnp.concatenate([high, low], axis=1)
    crossed = jnp.concatenate([low, high], axis=1)
    return jnp.concatenate([straight, crossed], axis=0)


def product(g_ref, u):
    cases = u.shape[1]
    wide = jnp.dot(g_ref[...], operand(u), preferred_element_type=F32)
    return wide[:, :cases] + wide[:, cases:]


def fine_product(g_ref, u):
    size, cases = u.shape
    high, low = halves(u)
    rest = (u - high.astype(F32) - low.astype(F32)).astype(BF16)
    wide = jnp.dot(g_ref[:, :size], jnp.concatenate([high, low], axis=1), preferred_element_type=F32)
    crossed = jnp.concatenate([jnp.concatenate([rest, jnp.zeros_like(rest)], axis=1), jnp.concatenate([high, low], axis=1)], axis=0)
    fine = jnp.dot(g_ref[...], crossed, preferred_element_type=F32)
    return wide[:, :cases] + (wide[:, cases:] + (fine[:, :cases] + fine[:, cases:]))


def rows_sum(x):
    return jnp.sum(x, axis=0, keepdims=True)


def take_in(info, u_ref, own, got):
    face = u_ref.shape[0] // 4
    for k in range(4):
        value = own[k][0:face, :] - got[k][0:face, :]
        if k < 2:
            value = jnp.where(info[KEEP + k] != 0, value, 0.0)
        u_ref[k * face : (k + 1) * face, :] = value


def hand_out(y, outs):
    face = y.shape[0] // 4
    for k, out in enumerate(outs):
        out[0:face, :] = y[k * face : (k + 1) * face]
        if out.shape[0] > face:
            out[face:, :] = jnp.zeros((out.shape[0] - face, out.shape[1]), F32)


def first_kernel(info, below, beside, rhs, g_ref, u_ref, a, b, c, d):
    face = rhs.shape[0] // 2
    own_up = jnp.where(info[KEEP + 2] != 0, rhs[0:face, :], 0.0)
    own_right = rhs[face:, :]
    minus_below = jnp.where(info[KEEP + 3] != 0, -below[0:face, :], 0.0)
    minus_beside = -beside[face:, :]
    odd_floor, odd_facade = info[ODD] != 0, info[ODD + 1] != 0
    u_ref[0:face, :] = jnp.where(odd_floor, minus_below, own_up)
    u_ref[face : 2 * face, :] = jnp.where(odd_floor, own_up, minus_below)
    u_ref[2 * face : 3 * face, :] = jnp.where(odd_facade, minus_beside, own_right)
    u_ref[3 * face :, :] = jnp.where(odd_facade, own_right, minus_beside)
    hand_out(product(g_ref, u_ref[...]), (a, b, c, d))


def next_kernel(fine, info, ya, yb, yc, yd, ra, rb, rc, rd, g_ref, u_ref, a, b, c, d):
    take_in(info, u_ref, (ya, yb, yc, yd), (ra, rb, rc, rd))
    hand_out((fine_product if fine else product)(g_ref, u_ref[...]), (a, b, c, d))


def differences(w, scale):
    values = []
    power = None
    for k, value in enumerate(w):
        values.append(value if k == 0 else value * power)
        power = scale if k == 0 else power * scale
    out = [values[0]]
    while len(values) > 1:
        values = [values[k + 1] - values[k] for k in range(len(values) - 1)]
        out.append(values[0])
    return out


def last_kernel(info, ya, yb, yc, yd, ra, rb, rc, rd, u0, u1, u2, *rest):
    ys, (center, g_ref, u_ref, down, left, yo_ref, node, y_ref) = rest[:8], rest[8:]
    ys = [ys[:4], ys[4:], (ya, yb, yc, yd)]
    take_in(info, u_ref, (ya, yb, yc, yd), (ra, rb, rc, rd))
    face = down.shape[0]
    y_ref[...] = fine_product(g_ref, u_ref[...])

    def rows(j):
        return pl.ds(pl.multiple_of(info[SLOT + j] * face, face), face)

    down[...] = y_ref[rows(0), :]
    left[...] = y_ref[rows(2), :]
    yo_ref[0:face, :] = y_ref[rows(1), :]
    yo_ref[face:, :] = y_ref[rows(3), :]

    middle = center[0:1, :]
    scale = 1.0 / middle
    sums = [jnp.zeros((8, down.shape[1]), F32)] * (2 * len(PAIRS))
    step = 16
    for k in range(4):
        for at in range(0, face, step):
            here, there = slice(at, at + step), slice(k * face + at, k * face + at + step)
            v = differences([u[there, :] for u in (u0, u1, u2, u_ref)], scale)
            f = differences([y[k][here, :] for y in ys] + [y_ref[there, :]], scale)
            for q, (i, j) in enumerate(PAIRS):
                for part, term in ((0, v[i] * v[j]), (1, v[j] * f[i])):
                    for m in range(0, step, 8):
                        sums[2 * q + part] = sums[2 * q + part] + term[m : m + 8]
    for q in range(len(PAIRS)):
        node[2 * q : 2 * q + 1, :] = 0.5 * rows_sum(sums[2 * q])
        node[2 * q + 1 : 2 * q + 2, :] = scale * rows_sum(sums[2 * q + 1])
    node[CENTER:NODE, :] = jnp.broadcast_to(middle, (NODE - CENTER, middle.shape[1]))


def tree(values):
    while len(values) > 1:
        values = [values[k] + values[k + 1] for k in range(0, len(values), 2)]
    return values[0]


BINOMIAL = ((1,), (1, 1), (1, 2, 1), (1, 3, 3, 1), (1, 4, 6, 4, 1))


def merged(parts):
    centers = [part[CENTER : CENTER + 1, :] for part in parts]
    middle = tree(centers) * (1.0 / len(parts))
    moved = []
    for part, center in zip(parts, centers):
        ratio = center / middle
        shift = (center - middle) / middle
        ratios, shifts = [None, ratio, ratio * ratio, ratio * ratio * ratio], [None, shift, shift * shift, shift * shift * shift]

        def entry(k, j):
            value = None
            for power in (ratios[j], shifts[k - j]):
                if power is not None:
                    value = power if value is None else value * power
            return value if BINOMIAL[k][j] == 1 or value is None else BINOMIAL[k][j] * value

        change = [[entry(k, j) for j in range(k + 1)] for k in range(4)]

        def times(factor, value):
            return value if factor is None else factor * value

        row = {}
        for q, (i, j) in enumerate(PAIRS):
            row[i, j] = row[j, i] = part[2 * q : 2 * q + 2, :]
        half = [[tree_any([times(change[k][j], row[j, m]) for j in range(k + 1)]) for m in range(4)] for k in range(4)]
        unit = jnp.concatenate([jnp.ones_like(ratio), ratio], axis=0)
        moved.append(
            [unit * tree_any([times(change[j][m], half[i][m]) for m in range(j + 1)]) for i, j in PAIRS]
        )
    return [tree([values[q] for values in moved]) for q in range(len(PAIRS))], middle


def tree_any(values):
    return functools.reduce(lambda a, b: a + b, values)


def write_node(node, rows, middle):
    for q in range(len(PAIRS)):
        node[2 * q : 2 * q + 2, :] = rows[q]
    node[CENTER:NODE, :] = jnp.broadcast_to(middle, (NODE - CENTER, middle.shape[1]))


def merge_kernel(*refs):
    parts, node = refs[:-1], refs[-1]
    write_node(node, *merged(parts))


def conjugate_coefficients(rows):
    inner, energy = {}, {}
    for q, pair in enumerate(PAIRS):
        inner[pair], energy[pair] = rows[q][0:1, :], rows[q][1:2, :]

    def square(a, matrix):
        terms = []
        for i in range(len(a)):
            mixed = [2.0 * (a[j] * matrix[i, j]) for j in range(i + 1, len(a))]
            terms.append(a[i] * tree_any([a[i] * matrix[i, i]] + mixed))
        return tree_any(terms)

    def plus(a, s, b):
        return [a[k] + s * b[k] if k < len(a) else s * b[k] for k in range(len(b))]

    one = jnp.ones_like(rows[0][0:1, :])
    x, r, p = [], [one], [one]
    norm = inner[0, 0]
    norms = [norm]
    for sweep in range(ITERS):
        step = norm / square(p, energy)
        x = plus(x, step, p)
        image = [p[0]] + [p[k] + p[k - 1] for k in range(1, len(p))] + [p[-1]]
        r = plus(r, -step, image)
        if sweep + 1 < ITERS:
            fresh = square(r, inner)
            p = plus(r, fresh / norm, p + [jnp.zeros_like(one)])
            norm = fresh
            norms.append(norm)
    return x, r, norms


def soundness(rows, norms, r):
    inner = {}
    for q, (i, j) in enumerate(PAIRS):
        inner[i, j] = inner[j, i] = rows[q][0:1, :]
    lengths = [
        tree_any([float(BINOMIAL[k][i] * BINOMIAL[k][j]) * inner[i, j] for i in range(k + 1) for j in range(k + 1)])
        for k in range(4)
    ]
    lengths.append(lengths[3] * (lengths[3] / lengths[2]))
    terms = tree_any([r[k] * r[k] * lengths[k] for k in range(5)])
    return jnp.where((terms <= GROWTH * norms[-1]) & (norms[-1] > 0.0), 1.0, 0.0)


def powers(coefficients, scale):
    out = []
    power = None
    for j in range(len(coefficients)):
        value = tree_any(
            [coefficients[k] * float(BINOMIAL[k][j] * (-1) ** (k - j)) for k in range(j, len(coefficients))]
        )
        out.append(value if power is None else value * power)
        power = scale if power is None else power * scale
    return out


def image_kernel(info, yo_ref, got_up, got_right, *rest):
    parts, (w4_ref, node) = rest[:-2], rest[-2:]
    face = got_up.shape[0]
    for f, got in enumerate((got_up, got_right)):
        rows = slice(f * face, (f + 1) * face)
        image = yo_ref[rows, :] - got[...]
        if f == 0:
            image = jnp.where(info[KEEP + 2] != 0, image, 0.0)
        w4_ref[rows, :] = image
    write_node(node, *merged(parts))


def final_kernel(info, u0, u1, u2, u3, yo_ref, got_up, got_right, *rest):
    parts, (mult, resid, sound) = rest[:-3], rest[-3:]
    rows, middle = merged(parts)
    scale = 1.0 / middle
    x, r, norms = conjugate_coefficients(rows)
    sound[0, 0] = jnp.min(soundness(rows, norms, powers(r, jnp.ones_like(scale)))).astype(jnp.int32)
    x = [value * scale for value in powers(x, scale)]
    r = powers(r, scale)
    face = got_up.shape[0]
    for f, got in enumerate((got_up, got_right)):
        place = pl.ds(pl.multiple_of(info[SLOT + 2 * f + 1] * face, face), face)
        here = slice(f * face, (f + 1) * face)
        w = [u[place, :] for u in (u0, u1, u2, u3)]
        image = yo_ref[here, :] - got[...]
        if f == 0:
            image = jnp.where(info[KEEP + 2] != 0, image, 0.0)
        mult[here, :] = x[0] * w[0] + x[1] * w[1] + x[2] * w[2] + x[3] * w[3]
        resid[here, :] = r[0] * w[0] + r[1] * w[1] + r[2] * w[2] + r[3] * w[3] + r[4] * image


def hand_on_kernel(mult_in, resid_in, mult, resid):
    mult[...] = mult_in[...]
    resid[...] = resid_in[...]


def upward(value, axis, steps, wrap):
    count = lax.axis_size(axis)
    pairs = [(i, (i + steps) % count) for i in range(count) if wrap or 0 <= i + steps < count]
    return lax.ppermute(value, axis, pairs)


def swapped(value, axis, odd, wrap):
    count = lax.axis_size(axis)
    pairs = []
    for i in range(odd, count, 2):
        if i + 1 < count or wrap:
            j = (i + 1) % count
            pairs += [(i, j), (j, i)]
    return lax.ppermute(value, axis, pairs)


def exchanged(a, b, c, d):
    d = swapped(d, "facade", 1, True)
    c = swapped(c, "facade", 0, True)
    b = swapped(b, "floor", 1, True)
    a = swapped(a, "floor", 0, False)
    return a, b, c, d


def flipped(value, flip_floor, flip_facade):
    floors, columns = lax.axis_size("floor"), lax.axis_size("facade")
    pairs = [
        (f * columns + c, (f ^ flip_floor) * columns + (c ^ flip_facade)) for f in range(floors) for c in range(columns)
    ]
    return lax.ppermute(value, AXES, pairs)


def sum_stages():
    floors, columns = lax.axis_size("floor"), lax.axis_size("facade")
    flips = []
    bit = 1
    while bit < floors:
        flips.append((bit, 0))
        bit *= 2
    bit = 1
    while bit < columns:
        flips.append((0, bit))
        bit *= 2
    return [flips[:1]] + [flips[k : k + 2] for k in range(1, len(flips), 2)]


def stage_parts(value, stage):
    if len(stage) == 1:
        return [value, flipped(value, *stage[0])]
    (f1, c1), (f2, c2) = stage
    return [value, flipped(value, f1 ^ f2, c1 ^ c2), flipped(value, f2, c2), flipped(value, f1, c1)]


def plain_iterations(rhs, factor, coupling, pattern, has_above):
    face, cases = rhs.shape[0] // 2, rhs.shape[1]
    size = 4 * face
    block = size // pattern.shape[0]
    expanded = jnp.repeat(jnp.repeat(pattern, block, axis=0), block, axis=1)
    masked = jnp.where(expanded != 0, coupling, jnp.zeros_like(coupling))
    top_keep = has_above.astype(F32)

    def dot(x, y, contract):
        return lax.dot_general(x, y, ((contract, (0,)), ((), ())), precision=lax.Precision.HIGHEST, preferred_element_type=F32)

    def image_of(v):
        up, right = v[:face], v[face:]
        below, beside = upward(up, "floor", 1, False), upward(right, "facade", 1, True)
        u = jnp.concatenate([-below, up, -beside, right], axis=0)
        y = dot(factor, dot(factor, u, (1,)), (0,))
        forward = dot(masked, u.astype(BF16), (1,)).astype(BF16)
        y = (y + dot(masked, forward, (0,))).reshape(4, face, cases)
        above, beyond = upward(y[0], "floor", -1, False), upward(y[2], "facade", -1, True)
        return jnp.concatenate([(y[1] - above) * top_keep, y[3] - beyond], axis=0)

    def inner(a, b):
        return lax.psum(jnp.sum(a * b, axis=0), AXES)

    def step(_, state):
        mult, resid, direction, norm = state
        image = image_of(direction)
        length = norm / inner(direction, image)
        mult = mult + length * direction
        resid = resid - length * image
        fresh = inner(resid, resid)
        return mult, resid, resid + fresh / norm * direction, fresh

    start = jnp.concatenate([rhs[:face] * top_keep, rhs[face:]], axis=0)
    state = (jnp.zeros_like(start), start, start, inner(start, start))
    return lax.fori_loop(0, ITERS, step, state)[:2]


MERGE_FLOPS = 3000000000
GROWTH = 1.0e6


def call(kernel, outs, scratch, smem, *args, flops=0):
    return pl.pallas_call(
        kernel,
        in_specs=[pl.BlockSpec(memory_space=pltpu.SMEM)] * smem
        + [pl.BlockSpec(memory_space=pltpu.VMEM)] * (len(args) - smem),
        out_specs=[pl.BlockSpec(memory_space=pltpu.VMEM)] * len(outs),
        out_shape=outs,
        scratch_shapes=scratch,
        compiler_params=params(16),
        cost_estimate=pl.CostEstimate(flops=flops, bytes_accessed=0, transcendentals=0) if flops else None,
    )(*args)


def finish(outs, info, *args):
    return pl.pallas_call(
        final_kernel,
        in_specs=[pl.BlockSpec(memory_space=pltpu.SMEM)] + [pl.BlockSpec(memory_space=pltpu.VMEM)] * len(args),
        out_specs=[pl.BlockSpec(memory_space=pltpu.VMEM)] * 2 + [pl.BlockSpec(memory_space=pltpu.SMEM)],
        out_shape=outs + [jax.ShapeDtypeStruct((1, 1), jnp.int32)],
        compiler_params=params(16),
    )(info, *args)


def local(interface_rhs, inverse_factor, near_coupling, near_pattern):
    face, cases = interface_rhs.shape[3:]
    size = 4 * face
    floors = lax.axis_size("floor")
    floor_pos, facade_pos = lax.axis_index("floor"), lax.axis_index("facade")
    odd_floor, odd_facade = floor_pos % 2, facade_pos % 2
    has_below = (floor_pos > 0).astype(jnp.int32)
    has_above = (floor_pos < floors - 1).astype(jnp.int32)
    keep_a = jnp.where(odd_floor == 0, has_above, has_below)
    keep_b = jnp.where(odd_floor == 0, has_below, has_above)
    flags = [1 - odd_floor, odd_floor, 3 - odd_facade, 2 + odd_facade, keep_a, keep_b, has_above, has_below, odd_floor, odd_facade]
    info = jnp.stack(flags).astype(jnp.int32)
    rhs = interface_rhs.reshape(2 * face, cases)
    beside = upward(rhs, "facade", 1, True)
    below = upward(rhs, "floor", 1, True)
    operator, center = build_operator(info, inverse_factor[0, 0], near_coupling[0, 0], near_pattern[0, 0], cases)

    def shaped(*dims):
        return jax.ShapeDtypeStruct(dims, F32)

    whole, part, node, owned = shaped(size, cases), shaped(face, cases), shaped(NODE, cases), shaped(2 * face, cases)
    sent = [shaped(face + rows, cases) for rows in PADS]

    u0, *y0 = call(first_kernel, [whole, *sent], [], 1, info, below, beside, rhs, operator)
    u1, *y1 = call(functools.partial(next_kernel, False), [whole, *sent], [], 1, info, *y0, *exchanged(*y0), operator)
    u2, *y2 = call(functools.partial(next_kernel, True), [whole, *sent], [], 1, info, *y1, *exchanged(*y1), operator)
    u3, y_down, y_left, y_own, total = call(
        last_kernel,
        [whole, part, part, owned, node],
        [pltpu.VMEM((size, cases), F32)],
        1,
        info, *y2, *exchanged(*y2), u0, u1, u2, *y0, *y1, center, operator,
    )
    got_right = upward(y_left, "facade", -1, True)
    got_up = upward(y_down, "floor", -1, True)
    *stages, before, last = sum_stages()
    for stage in stages + [before]:
        (total,) = call(merge_kernel, [node], [], 0, *stage_parts(total, stage), flops=MERGE_FLOPS if stage is before else 0)
    mult, resid, sound = finish([owned, owned], info, u0, u1, u2, u3, y_own, got_up, got_right, *stage_parts(total, last))
    def one_by_one(state):
        result = plain_iterations(rhs, inverse_factor[0, 0], near_coupling[0, 0], near_pattern[0, 0], has_above)
        return (*call(hand_on_kernel, [owned, owned], [], 0, *result), jnp.int32(1))

    mult, resid, _ = lax.while_loop(lambda state: state[2] == 0, one_by_one, (mult, resid, sound[0, 0]))
    shape = (1, 1, 2, face, cases)
    return mult.reshape(shape), resid.reshape(shape)


def solution(mesh):
    spec = P("floor", "facade", None, None, None)
    flat = P("floor", "facade", None, None)
    return jax.shard_map(
        local,
        mesh=mesh,
        in_specs=(spec, flat, flat, flat),
        out_specs=(spec, spec),
        check_vma=False,
    )
```

```python
import functools

import jax
import jax.numpy as jnp
from jax import lax
from jax.experimental import pallas as pl
from jax.experimental.pallas import tpu as pltpu
from jax.sharding import PartitionSpec as P

ITERS = 4
SLOT, KEEP, ODD = 0, 4, 8
PADS = (8, 0, 24, 16)
PAIRS = [(i, j) for i in range(4) for j in range(i, 4)]
CENTER, NODE = 20, 24
AXES = ("floor", "facade")
F32 = jnp.float32
BF16 = jnp.bfloat16


def halves(x):
    high = x.astype(BF16)
    return high, (x - high.astype(F32)).astype(BF16)


def params(mib):
    return pltpu.CompilerParams(vmem_limit_bytes=mib << 20)


def operator_kernel(info, pattern_hbm, w_hbm, n_hbm, g_ref, center_ref, pattern, w_buf, n_buf, sems, left, right, total):
    size = w_buf.shape[1]
    face = size // 4
    nb = pattern.shape[0]
    blk = size // nb
    pattern_copy = pltpu.make_async_copy(pattern_hbm, pattern, sems.at[2, 0])
    pattern_copy.start()

    def fetch(k):
        rows = pl.ds(k * face, face)
        return (
            pltpu.make_async_copy(w_hbm.at[rows, :], w_buf.at[rows, :], sems.at[0, k]),
            pltpu.make_async_copy(n_hbm.at[rows, :], n_buf.at[rows, :], sems.at[1, k]),
        )

    def prepare(k):
        for copy in fetch(k):
            copy.wait()
        begin(k + 2)
        high, low = halves(w_buf[k * face : (k + 1) * face, :])
        here, there = left.at[k % 2], right.at[k % 2]
        there[0:face, :] = high
        there[face : 2 * face, :] = low
        there[2 * face : 3 * face, :] = high
        for a in range(face // blk):
            for b in range(nb):
                keep = pattern[k * (face // blk) + a, b] != 0
                cols = slice(b * blk, (b + 1) * blk)
                block = n_buf[k * face + a * blk : k * face + (a + 1) * blk, cols]
                there[3 * face + a * blk : 3 * face + (a + 1) * blk, cols] = jnp.where(
                    keep, block, jnp.zeros_like(block)
                )
        high_t = high.T
        here[:, 0:face] = high_t
        here[:, face : 2 * face] = high_t
        here[:, 2 * face : 3 * face] = low.T
        here[:, 3 * face :] = there[3 * face :, :].T

    def multiply(k):
        for i in range(4):
            rows, cols = slice(i * face, (i + 1) * face), slice(i * face, size)
            part = jnp.dot(left[k % 2, rows, :], right[k % 2, :, cols], preferred_element_type=F32)
            if k == 0:
                total[rows, cols] = part
            else:
                total[rows, cols] += part

    def begin(k):
        if k < 4:
            for copy in fetch(k):
                copy.start()

    begin(0)
    begin(1)
    pattern_copy.wait()
    prepare(0)
    for k in range(4):
        multiply(k)
        if k < 3:
            prepare(k + 1)

    def put(i, j, block):
        def at(k):
            return pl.multiple_of(info[k] * face, face)

        rows = pl.ds(at(i), face)
        high, low = halves(block)
        g_ref[rows, pl.ds(at(j), face)] = high
        g_ref[rows, pl.ds(pl.multiple_of(size + at(j), face), face)] = low

    diagonal = lax.broadcasted_iota(jnp.int32, (face, face), 0) == lax.broadcasted_iota(jnp.int32, (face, face), 1)
    trace = jnp.zeros((1, face), F32)
    for i in range(4):
        for j in range(i, 4):
            block = total[i * face : (i + 1) * face, j * face : (j + 1) * face]
            put(i, j, block)
            if j == i:
                trace = trace + rows_sum(jnp.where(diagonal, block, 0.0))
            if j > i:
                put(j, i, block.T)


    center_ref[...] = jnp.broadcast_to(jnp.sum(trace, axis=1, keepdims=True) * (2.0 / size), center_ref.shape)


def build_operator(info, factor, coupling, pattern, cases):
    size = factor.shape[0]
    return pl.pallas_call(
        operator_kernel,
        in_specs=[pl.BlockSpec(memory_space=pltpu.SMEM)] + [pl.BlockSpec(memory_space=pl.ANY)] * 3,
        out_specs=[pl.BlockSpec(memory_space=pltpu.VMEM)] * 2,
        out_shape=[jax.ShapeDtypeStruct((size, 2 * size), BF16), jax.ShapeDtypeStruct((8, cases), F32)],
        scratch_shapes=[
            pltpu.SMEM(pattern.shape, jnp.int32),
            pltpu.VMEM((size, size), F32),
            pltpu.VMEM((size, size), BF16),
            pltpu.SemaphoreType.DMA((3, 4)),
            pltpu.VMEM((2, size, size), BF16),
            pltpu.VMEM((2, size, size), BF16),
            pltpu.VMEM((size, size), F32),
        ],
        compiler_params=params(32),
        name="operator",
    )(
        info,
        pltpu.with_memory_space_constraint(pattern, pltpu.HBM),
        pltpu.with_memory_space_constraint(factor, pltpu.HBM),
        pltpu.with_memory_space_constraint(coupling, pltpu.HBM),
    )


def operand(u):
    high, low = halves(u)
    straight = jnp.concatenate([high, low], axis=1)
    crossed = jnp.concatenate([low, high], axis=1)
    return jnp.concatenate([straight, crossed], axis=0)


def product(g_ref, u):
    cases = u.shape[1]
    wide = jnp.dot(g_ref[...], operand(u), preferred_element_type=F32)
    return wide[:, :cases] + wide[:, cases:]


def fine_product(g_ref, u):
    size, cases = u.shape
    high, low = halves(u)
    rest = (u - high.astype(F32) - low.astype(F32)).astype(BF16)
    wide = jnp.dot(g_ref[:, :size], jnp.concatenate([high, low], axis=1), preferred_element_type=F32)
    crossed = jnp.concatenate([jnp.concatenate([rest, jnp.zeros_like(rest)], axis=1), jnp.concatenate([high, low], axis=1)], axis=0)
    fine = jnp.dot(g_ref[...], crossed, preferred_element_type=F32)
    return wide[:, :cases] + (wide[:, cases:] + (fine[:, :cases] + fine[:, cases:]))


def rows_sum(x):
    return jnp.sum(x, axis=0, keepdims=True)


def take_in(info, u_ref, own, got):
    face = u_ref.shape[0] // 4
    for k in range(4):
        value = own[k][0:face, :] - got[k][0:face, :]
        if k < 2:
            value = jnp.where(info[KEEP + k] != 0, value, 0.0)
        u_ref[k * face : (k + 1) * face, :] = value


def hand_out(y, outs):
    face = y.shape[0] // 4
    for k, out in enumerate(outs):
        out[0:face, :] = y[k * face : (k + 1) * face]
        if out.shape[0] > face:
            out[face:, :] = jnp.zeros((out.shape[0] - face, out.shape[1]), F32)


def first_kernel(info, below, beside, rhs, g_ref, u_ref, a, b, c, d):
    face = rhs.shape[0] // 2
    own_up = jnp.where(info[KEEP + 2] != 0, rhs[0:face, :], 0.0)
    own_right = rhs[face:, :]
    minus_below = jnp.where(info[KEEP + 3] != 0, -below[0:face, :], 0.0)
    minus_beside = -beside[face:, :]
    odd_floor, odd_facade = info[ODD] != 0, info[ODD + 1] != 0
    u_ref[0:face, :] = jnp.where(odd_floor, minus_below, own_up)
    u_ref[face : 2 * face, :] = jnp.where(odd_floor, own_up, minus_below)
    u_ref[2 * face : 3 * face, :] = jnp.where(odd_facade, minus_beside, own_right)
    u_ref[3 * face :, :] = jnp.where(odd_facade, own_right, minus_beside)
    hand_out(product(g_ref, u_ref[...]), (a, b, c, d))


def next_kernel(fine, info, ya, yb, yc, yd, ra, rb, rc, rd, g_ref, u_ref, a, b, c, d):
    take_in(info, u_ref, (ya, yb, yc, yd), (ra, rb, rc, rd))
    hand_out((fine_product if fine else product)(g_ref, u_ref[...]), (a, b, c, d))


def differences(w, scale):
    values = []
    power = None
    for k, value in enumerate(w):
        values.append(value if k == 0 else value * power)
        power = scale if k == 0 else power * scale
    out = [values[0]]
    while len(values) > 1:
        values = [values[k + 1] - values[k] for k in range(len(values) - 1)]
        out.append(values[0])
    return out


def shares(us, ys, scale, pairs):
    face = us[0].shape[0] // 4
    sums = [jnp.zeros((8, us[0].shape[1]), F32)] * (2 * len(pairs))
    step = 16
    for k in range(4):
        for at in range(0, face, step):
            here, there = slice(at, at + step), slice(k * face + at, k * face + at + step)
            v = differences([u[there, :] for u in us], scale)
            f = differences([y[k][here, :] for y in ys], scale)
            for q, (i, j) in enumerate(pairs):
                for part, term in ((0, v[i] * v[j]), (1, v[j] * f[i])):
                    for m in range(0, step, 8):
                        sums[2 * q + part] = sums[2 * q + part] + term[m : m + 8]
    return [rows_sum(value) * (scale if k % 2 else 0.5) for k, value in enumerate(sums)]


def early_shares_kernel(u0, u1, u2, *rest):
    ys, (center, out) = rest[:12], rest[12:]
    pairs = [pair for pair in PAIRS if pair[1] < 3]
    values = shares((u0, u1, u2), (ys[:4], ys[4:8], ys[8:]), 1.0 / center[0:1, :], pairs)
    out[...] = jnp.zeros_like(out)
    for k, value in enumerate(values):
        out[k : k + 1, :] = value


def last_kernel(info, ya, yb, yc, yd, ra, rb, rc, rd, u0, u1, u2, *rest):
    ys, (early, center, g_ref, u_ref, down, left, yo_ref, node, y_ref) = rest[:8], rest[8:]
    take_in(info, u_ref, (ya, yb, yc, yd), (ra, rb, rc, rd))
    face = down.shape[0]
    y_ref[...] = fine_product(g_ref, u_ref[...])

    def rows(j):
        return pl.ds(pl.multiple_of(info[SLOT + j] * face, face), face)

    down[...] = y_ref[rows(0), :]
    left[...] = y_ref[rows(2), :]
    yo_ref[0:face, :] = y_ref[rows(1), :]
    yo_ref[face:, :] = y_ref[rows(3), :]

    middle = center[0:1, :]
    y3 = tuple(y_ref.at[k * face : (k + 1) * face, :] for k in range(4))
    pairs = [pair for pair in PAIRS if pair[1] == 3]
    values = shares((u0, u1, u2, u_ref), (ys[:4], ys[4:], (ya, yb, yc, yd), y3), 1.0 / middle, pairs)
    at_early = at_late = 0
    for q, pair in enumerate(PAIRS):
        here = slice(2 * q, 2 * q + 2)
        if pair[1] < 3:
            node[here, :] = early[2 * at_early : 2 * at_early + 2, :]
            at_early += 1
        else:
            node[here, :] = jnp.concatenate(values[2 * at_late : 2 * at_late + 2], axis=0)
            at_late += 1
    node[CENTER:NODE, :] = jnp.broadcast_to(middle, (NODE - CENTER, middle.shape[1]))


def tree(values):
    while len(values) > 1:
        values = [values[k] + values[k + 1] for k in range(0, len(values), 2)]
    return values[0]


BINOMIAL = ((1,), (1, 1), (1, 2, 1), (1, 3, 3, 1), (1, 4, 6, 4, 1))


def merged(parts):
    centers = [part[CENTER : CENTER + 1, :] for part in parts]
    middle = tree(centers) * (1.0 / len(parts))
    moved = []
    for part, center in zip(parts, centers):
        ratio = center / middle
        shift = (center - middle) / middle
        ratios, shifts = [None, ratio, ratio * ratio, ratio * ratio * ratio], [None, shift, shift * shift, shift * shift * shift]

        def entry(k, j):
            value = None
            for power in (ratios[j], shifts[k - j]):
                if power is not None:
                    value = power if value is None else value * power
            return value if BINOMIAL[k][j] == 1 or value is None else BINOMIAL[k][j] * value

        change = [[entry(k, j) for j in range(k + 1)] for k in range(4)]

        def times(factor, value):
            return value if factor is None else factor * value

        row = {}
        for q, (i, j) in enumerate(PAIRS):
            row[i, j] = row[j, i] = part[2 * q : 2 * q + 2, :]
        half = [[tree_any([times(change[k][j], row[j, m]) for j in range(k + 1)]) for m in range(4)] for k in range(4)]
        unit = jnp.concatenate([jnp.ones_like(ratio), ratio], axis=0)
        moved.append(
            [unit * tree_any([times(change[j][m], half[i][m]) for m in range(j + 1)]) for i, j in PAIRS]
        )
    return [tree([values[q] for values in moved]) for q in range(len(PAIRS))], middle


def tree_any(values):
    return functools.reduce(lambda a, b: a + b, values)


def write_node(node, rows, middle):
    for q in range(len(PAIRS)):
        node[2 * q : 2 * q + 2, :] = rows[q]
    node[CENTER:NODE, :] = jnp.broadcast_to(middle, (NODE - CENTER, middle.shape[1]))


def merge_kernel(*refs):
    parts, node = refs[:-1], refs[-1]
    write_node(node, *merged(parts))


def conjugate_coefficients(rows):
    inner, energy = {}, {}
    for q, pair in enumerate(PAIRS):
        inner[pair], energy[pair] = rows[q][0:1, :], rows[q][1:2, :]

    def square(a, matrix):
        terms = []
        for i in range(len(a)):
            mixed = [2.0 * (a[j] * matrix[i, j]) for j in range(i + 1, len(a))]
            terms.append(a[i] * tree_any([a[i] * matrix[i, i]] + mixed))
        return tree_any(terms)

    def plus(a, s, b):
        return [a[k] + s * b[k] if k < len(a) else s * b[k] for k in range(len(b))]

    one = jnp.ones_like(rows[0][0:1, :])
    x, r, p = [], [one], [one]
    norm = inner[0, 0]
    norms = [norm]
    for sweep in range(ITERS):
        step = norm / square(p, energy)
        x = plus(x, step, p)
        image = [p[0]] + [p[k] + p[k - 1] for k in range(1, len(p))] + [p[-1]]
        r = plus(r, -step, image)
        if sweep + 1 < ITERS:
            fresh = square(r, inner)
            p = plus(r, fresh / norm, p + [jnp.zeros_like(one)])
            norm = fresh
            norms.append(norm)
    return x, r, norms


def soundness(rows, norms, r):
    inner = {}
    for q, (i, j) in enumerate(PAIRS):
        inner[i, j] = inner[j, i] = rows[q][0:1, :]
    lengths = [
        tree_any([float(BINOMIAL[k][i] * BINOMIAL[k][j]) * inner[i, j] for i in range(k + 1) for j in range(k + 1)])
        for k in range(4)
    ]
    lengths.append(lengths[3] * (lengths[3] / lengths[2]))
    terms = tree_any([r[k] * r[k] * lengths[k] for k in range(5)])
    return jnp.where((terms <= GROWTH * norms[-1]) & (norms[-1] > 0.0), 1.0, 0.0)


def powers(coefficients, scale):
    out = []
    power = None
    for j in range(len(coefficients)):
        value = tree_any(
            [coefficients[k] * float(BINOMIAL[k][j] * (-1) ** (k - j)) for k in range(j, len(coefficients))]
        )
        out.append(value if power is None else value * power)
        power = scale if power is None else power * scale
    return out


def image_kernel(info, yo_ref, got_up, got_right, *rest):
    parts, (w4_ref, node) = rest[:-2], rest[-2:]
    face = got_up.shape[0]
    for f, got in enumerate((got_up, got_right)):
        rows = slice(f * face, (f + 1) * face)
        image = yo_ref[rows, :] - got[...]
        if f == 0:
            image = jnp.where(info[KEEP + 2] != 0, image, 0.0)
        w4_ref[rows, :] = image
    write_node(node, *merged(parts))


def final_kernel(info, u0, u1, u2, u3, yo_ref, got_up, got_right, *rest):
    parts, (mult, resid, sound) = rest[:-3], rest[-3:]
    rows, middle = merged(parts)
    scale = 1.0 / middle
    x, r, norms = conjugate_coefficients(rows)
    sound[0, 0] = jnp.min(soundness(rows, norms, powers(r, jnp.ones_like(scale)))).astype(jnp.int32)
    x = [value * scale for value in powers(x, scale)]
    r = powers(r, scale)
    face = got_up.shape[0]
    for f, got in enumerate((got_up, got_right)):
        place = pl.ds(pl.multiple_of(info[SLOT + 2 * f + 1] * face, face), face)
        here = slice(f * face, (f + 1) * face)
        w = [u[place, :] for u in (u0, u1, u2, u3)]
        image = yo_ref[here, :] - got[...]
        if f == 0:
            image = jnp.where(info[KEEP + 2] != 0, image, 0.0)
        mult[here, :] = x[0] * w[0] + x[1] * w[1] + x[2] * w[2] + x[3] * w[3]
        resid[here, :] = r[0] * w[0] + r[1] * w[1] + r[2] * w[2] + r[3] * w[3] + r[4] * image


def hand_on_kernel(mult_in, resid_in, mult, resid):
    mult[...] = mult_in[...]
    resid[...] = resid_in[...]


def upward(value, axis, steps, wrap):
    count = lax.axis_size(axis)
    pairs = [(i, (i + steps) % count) for i in range(count) if wrap or 0 <= i + steps < count]
    return lax.ppermute(value, axis, pairs)


def swapped(value, axis, odd, wrap):
    count = lax.axis_size(axis)
    pairs = []
    for i in range(odd, count, 2):
        if i + 1 < count or wrap:
            j = (i + 1) % count
            pairs += [(i, j), (j, i)]
    return lax.ppermute(value, axis, pairs)


def exchanged(a, b, c, d):
    d = swapped(d, "facade", 1, True)
    c = swapped(c, "facade", 0, True)
    b = swapped(b, "floor", 1, True)
    a = swapped(a, "floor", 0, False)
    return a, b, c, d


def flipped(value, flip_floor, flip_facade):
    floors, columns = lax.axis_size("floor"), lax.axis_size("facade")
    pairs = [
        (f * columns + c, (f ^ flip_floor) * columns + (c ^ flip_facade)) for f in range(floors) for c in range(columns)
    ]
    return lax.ppermute(value, AXES, pairs)


def sum_stages():
    floors, columns = lax.axis_size("floor"), lax.axis_size("facade")
    flips = []
    bit = 1
    while bit < floors:
        flips.append((bit, 0))
        bit *= 2
    bit = 1
    while bit < columns:
        flips.append((0, bit))
        bit *= 2
    return [flips[:1]] + [flips[k : k + 2] for k in range(1, len(flips), 2)]


def stage_parts(value, stage):
    if len(stage) == 1:
        return [value, flipped(value, *stage[0])]
    (f1, c1), (f2, c2) = stage
    return [value, flipped(value, f1 ^ f2, c1 ^ c2), flipped(value, f2, c2), flipped(value, f1, c1)]


def plain_iterations(rhs, factor, coupling, pattern, has_above):
    face, cases = rhs.shape[0] // 2, rhs.shape[1]
    size = 4 * face
    block = size // pattern.shape[0]
    expanded = jnp.repeat(jnp.repeat(pattern, block, axis=0), block, axis=1)
    masked = jnp.where(expanded != 0, coupling, jnp.zeros_like(coupling))
    top_keep = has_above.astype(F32)

    def dot(x, y, contract):
        return lax.dot_general(x, y, ((contract, (0,)), ((), ())), precision=lax.Precision.HIGHEST, preferred_element_type=F32)

    def image_of(v):
        up, right = v[:face], v[face:]
        below, beside = upward(up, "floor", 1, False), upward(right, "facade", 1, True)
        u = jnp.concatenate([-below, up, -beside, right], axis=0)
        y = dot(factor, dot(factor, u, (1,)), (0,))
        forward = dot(masked, u.astype(BF16), (1,)).astype(BF16)
        y = (y + dot(masked, forward, (0,))).reshape(4, face, cases)
        above, beyond = upward(y[0], "floor", -1, False), upward(y[2], "facade", -1, True)
        return jnp.concatenate([(y[1] - above) * top_keep, y[3] - beyond], axis=0)

    def inner(a, b):
        return lax.psum(jnp.sum(a * b, axis=0), AXES)

    def step(_, state):
        mult, resid, direction, norm = state
        image = image_of(direction)
        length = norm / inner(direction, image)
        mult = mult + length * direction
        resid = resid - length * image
        fresh = inner(resid, resid)
        return mult, resid, resid + fresh / norm * direction, fresh

    start = jnp.concatenate([rhs[:face] * top_keep, rhs[face:]], axis=0)
    state = (jnp.zeros_like(start), start, start, inner(start, start))
    return lax.fori_loop(0, ITERS, step, state)[:2]


MERGE_FLOPS = 3000000000
GROWTH = 1.0e6


def call(kernel, outs, scratch, smem, *args, flops=0):
    return pl.pallas_call(
        kernel,
        in_specs=[pl.BlockSpec(memory_space=pltpu.SMEM)] * smem
        + [pl.BlockSpec(memory_space=pltpu.VMEM)] * (len(args) - smem),
        out_specs=[pl.BlockSpec(memory_space=pltpu.VMEM)] * len(outs),
        out_shape=outs,
        scratch_shapes=scratch,
        compiler_params=params(16),
        cost_estimate=pl.CostEstimate(flops=flops, bytes_accessed=0, transcendentals=0) if flops else None,
    )(*args)


def finish(outs, info, *args):
    return pl.pallas_call(
        final_kernel,
        in_specs=[pl.BlockSpec(memory_space=pltpu.SMEM)] + [pl.BlockSpec(memory_space=pltpu.VMEM)] * len(args),
        out_specs=[pl.BlockSpec(memory_space=pltpu.VMEM)] * 2 + [pl.BlockSpec(memory_space=pltpu.SMEM)],
        out_shape=outs + [jax.ShapeDtypeStruct((1, 1), jnp.int32)],
        compiler_params=params(16),
    )(info, *args)


def local(interface_rhs, inverse_factor, near_coupling, near_pattern):
    face, cases = interface_rhs.shape[3:]
    size = 4 * face
    floors = lax.axis_size("floor")
    floor_pos, facade_pos = lax.axis_index("floor"), lax.axis_index("facade")
    odd_floor, odd_facade = floor_pos % 2, facade_pos % 2
    has_below = (floor_pos > 0).astype(jnp.int32)
    has_above = (floor_pos < floors - 1).astype(jnp.int32)
    keep_a = jnp.where(odd_floor == 0, has_above, has_below)
    keep_b = jnp.where(odd_floor == 0, has_below, has_above)
    flags = [1 - odd_floor, odd_floor, 3 - odd_facade, 2 + odd_facade, keep_a, keep_b, has_above, has_below, odd_floor, odd_facade]
    info = jnp.stack(flags).astype(jnp.int32)
    rhs = interface_rhs.reshape(2 * face, cases)
    beside = upward(rhs, "facade", 1, True)
    below = upward(rhs, "floor", 1, True)
    operator, center = build_operator(info, inverse_factor[0, 0], near_coupling[0, 0], near_pattern[0, 0], cases)

    def shaped(*dims):
        return jax.ShapeDtypeStruct(dims, F32)

    whole, part, node, owned = shaped(size, cases), shaped(face, cases), shaped(NODE, cases), shaped(2 * face, cases)
    sent = [shaped(face + rows, cases) for rows in PADS]

    u0, *y0 = call(first_kernel, [whole, *sent], [], 1, info, below, beside, rhs, operator)
    u1, *y1 = call(functools.partial(next_kernel, False), [whole, *sent], [], 1, info, *y0, *exchanged(*y0), operator)
    u2, *y2 = call(functools.partial(next_kernel, True), [whole, *sent], [], 1, info, *y1, *exchanged(*y1), operator)
    (early,) = call(early_shares_kernel, [shaped(16, cases)], [], 0, u0, u1, u2, *y0, *y1, *y2, center)
    u3, y_down, y_left, y_own, total = call(
        last_kernel,
        [whole, part, part, owned, node],
        [pltpu.VMEM((size, cases), F32)],
        1,
        info, *y2, *exchanged(*y2), u0, u1, u2, *y0, *y1, early, center, operator,
    )
    got_right = upward(y_left, "facade", -1, True)
    got_up = upward(y_down, "floor", -1, True)
    *stages, before, last = sum_stages()
    for stage in stages + [before]:
        (total,) = call(merge_kernel, [node], [], 0, *stage_parts(total, stage), flops=MERGE_FLOPS if stage is before else 0)
    mult, resid, sound = finish([owned, owned], info, u0, u1, u2, u3, y_own, got_up, got_right, *stage_parts(total, last))
    def one_by_one(state):
        result = plain_iterations(rhs, inverse_factor[0, 0], near_coupling[0, 0], near_pattern[0, 0], has_above)
        return (*call(hand_on_kernel, [owned, owned], [], 0, *result), jnp.int32(1))

    mult, resid, _ = lax.while_loop(lambda state: state[2] == 0, one_by_one, (mult, resid, sound[0, 0]))
    shape = (1, 1, 2, face, cases)
    return mult.reshape(shape), resid.reshape(shape)


def solution(mesh):
    spec = P("floor", "facade", None, None, None)
    flat = P("floor", "facade", None, None)
    return jax.shard_map(
        local,
        mesh=mesh,
        in_specs=(spec, flat, flat, flat),
        out_specs=(spec, spec),
        check_vma=False,
    )
```

```python
import functools

import jax
import jax.numpy as jnp
from jax import lax
from jax.experimental import pallas as pl
from jax.experimental.pallas import tpu as pltpu
from jax.sharding import PartitionSpec as P

ITERS = 4
SLOT, KEEP, ODD = 0, 4, 8
KEEP_A, KEEP_B, ABOVE, BELOW, ODD_FLOOR, ODD_FACADE = range(6)
PADS = (8, 0, 24, 16)
PAIRS = [(i, j) for i in range(4) for j in range(i, 4)]
CENTER, NODE = 20, 24
AXES = ("floor", "facade")
F32 = jnp.float32
BF16 = jnp.bfloat16


def halves(x):
    high = x.astype(BF16)
    return high, (x - high.astype(F32)).astype(BF16)


def params(mib):
    return pltpu.CompilerParams(vmem_limit_bytes=mib << 20)


def operator_kernel(info, pattern_hbm, w_hbm, n_hbm, g_ref, center_ref, pattern, w_buf, n_buf, sems, left, right, total):
    size = w_buf.shape[1]
    face = size // 4
    nb = pattern.shape[0]
    blk = size // nb
    pattern_copy = pltpu.make_async_copy(pattern_hbm, pattern, sems.at[2, 0])
    pattern_copy.start()

    def fetch(k):
        rows = pl.ds(k * face, face)
        return (
            pltpu.make_async_copy(w_hbm.at[rows, :], w_buf.at[rows, :], sems.at[0, k]),
            pltpu.make_async_copy(n_hbm.at[rows, :], n_buf.at[rows, :], sems.at[1, k]),
        )

    def prepare(k):
        for copy in fetch(k):
            copy.wait()
        begin(k + 2)
        high, low = halves(w_buf[k * face : (k + 1) * face, :])
        here, there = left.at[k % 2], right.at[k % 2]
        there[0:face, :] = high
        there[face : 2 * face, :] = low
        there[2 * face : 3 * face, :] = high
        for a in range(face // blk):
            for b in range(nb):
                keep = pattern[k * (face // blk) + a, b] != 0
                cols = slice(b * blk, (b + 1) * blk)
                block = n_buf[k * face + a * blk : k * face + (a + 1) * blk, cols]
                there[3 * face + a * blk : 3 * face + (a + 1) * blk, cols] = jnp.where(
                    keep, block, jnp.zeros_like(block)
                )
        high_t = high.T
        here[:, 0:face] = high_t
        here[:, face : 2 * face] = high_t
        here[:, 2 * face : 3 * face] = low.T
        here[:, 3 * face :] = there[3 * face :, :].T

    def multiply(k):
        for i in range(4):
            rows, cols = slice(i * face, (i + 1) * face), slice(i * face, size)
            part = jnp.dot(left[k % 2, rows, :], right[k % 2, :, cols], preferred_element_type=F32)
            if k == 0:
                total[rows, cols] = part
            else:
                total[rows, cols] += part

    def begin(k):
        if k < 4:
            for copy in fetch(k):
                copy.start()

    begin(0)
    begin(1)
    pattern_copy.wait()
    prepare(0)
    for k in range(4):
        multiply(k)
        if k < 3:
            prepare(k + 1)

    def put(i, j, block):
        def at(k):
            return pl.multiple_of(info[k] * face, face)

        rows = pl.ds(at(i), face)
        high, low = halves(block)
        g_ref[rows, pl.ds(at(j), face)] = high
        g_ref[rows, pl.ds(pl.multiple_of(size + at(j), face), face)] = low

    diagonal = lax.broadcasted_iota(jnp.int32, (face, face), 0) == lax.broadcasted_iota(jnp.int32, (face, face), 1)
    trace = jnp.zeros((1, face), F32)
    for i in range(4):
        for j in range(i, 4):
            block = total[i * face : (i + 1) * face, j * face : (j + 1) * face]
            put(i, j, block)
            if j == i:
                trace = trace + rows_sum(jnp.where(diagonal, block, 0.0))
            if j > i:
                put(j, i, block.T)


    center_ref[...] = jnp.broadcast_to(jnp.sum(trace, axis=1, keepdims=True) * (2.0 / size), center_ref.shape)


def build_operator(info, factor, coupling, pattern, cases):
    size = factor.shape[0]
    return pl.pallas_call(
        operator_kernel,
        in_specs=[pl.BlockSpec(memory_space=pltpu.SMEM)] + [pl.BlockSpec(memory_space=pl.ANY)] * 3,
        out_specs=[pl.BlockSpec(memory_space=pltpu.VMEM)] * 2,
        out_shape=[jax.ShapeDtypeStruct((size, 2 * size), BF16), jax.ShapeDtypeStruct((8, cases), F32)],
        scratch_shapes=[
            pltpu.SMEM(pattern.shape, jnp.int32),
            pltpu.VMEM((size, size), F32),
            pltpu.VMEM((size, size), BF16),
            pltpu.SemaphoreType.DMA((3, 4)),
            pltpu.VMEM((2, size, size), BF16),
            pltpu.VMEM((2, size, size), BF16),
            pltpu.VMEM((size, size), F32),
        ],
        compiler_params=params(32),
        name="operator",
    )(
        info,
        pltpu.with_memory_space_constraint(pattern, pltpu.HBM),
        pltpu.with_memory_space_constraint(factor, pltpu.HBM),
        pltpu.with_memory_space_constraint(coupling, pltpu.HBM),
    )


def operand(u):
    high, low = halves(u)
    straight = jnp.concatenate([high, low], axis=1)
    crossed = jnp.concatenate([low, high], axis=1)
    return jnp.concatenate([straight, crossed], axis=0)


def product(g_ref, u):
    cases = u.shape[1]
    wide = jnp.dot(g_ref[...], operand(u), preferred_element_type=F32)
    return wide[:, :cases] + wide[:, cases:]


def fine_product(g_ref, u):
    size, cases = u.shape
    high, low = halves(u)
    rest = (u - high.astype(F32) - low.astype(F32)).astype(BF16)
    wide = jnp.dot(g_ref[:, :size], jnp.concatenate([high, low], axis=1), preferred_element_type=F32)
    crossed = jnp.concatenate([jnp.concatenate([rest, jnp.zeros_like(rest)], axis=1), jnp.concatenate([high, low], axis=1)], axis=0)
    fine = jnp.dot(g_ref[...], crossed, preferred_element_type=F32)
    return wide[:, :cases] + (wide[:, cases:] + (fine[:, :cases] + fine[:, cases:]))


def rows_sum(x):
    return jnp.sum(x, axis=0, keepdims=True)


def holds(facts, row):
    return facts[row : row + 1, :] > 0.5


def take_in(facts, u_ref, own, got):
    face = u_ref.shape[0] // 4
    for k in range(4):
        value = own[k][0:face, :] - got[k][0:face, :]
        if k < 2:
            value = jnp.where(holds(facts, KEEP_A + k), value, 0.0)
        u_ref[k * face : (k + 1) * face, :] = value


def hand_out(y, outs):
    face = y.shape[0] // 4
    for k, out in enumerate(outs):
        out[0:face, :] = y[k * face : (k + 1) * face]
        if out.shape[0] > face:
            out[face:, :] = jnp.zeros((out.shape[0] - face, out.shape[1]), F32)


def first_kernel(facts, below, beside, rhs, g_ref, u_ref, a, b, c, d):
    face = rhs.shape[0] // 2
    own_up = jnp.where(holds(facts, ABOVE), rhs[0:face, :], 0.0)
    own_right = rhs[face:, :]
    minus_below = jnp.where(holds(facts, BELOW), -below[0:face, :], 0.0)
    minus_beside = -beside[face:, :]
    odd_floor, odd_facade = holds(facts, ODD_FLOOR), holds(facts, ODD_FACADE)
    u_ref[0:face, :] = jnp.where(odd_floor, minus_below, own_up)
    u_ref[face : 2 * face, :] = jnp.where(odd_floor, own_up, minus_below)
    u_ref[2 * face : 3 * face, :] = jnp.where(odd_facade, minus_beside, own_right)
    u_ref[3 * face :, :] = jnp.where(odd_facade, own_right, minus_beside)
    hand_out(product(g_ref, u_ref[...]), (a, b, c, d))


def next_kernel(fine, facts, ya, yb, yc, yd, ra, rb, rc, rd, g_ref, u_ref, a, b, c, d):
    take_in(facts, u_ref, (ya, yb, yc, yd), (ra, rb, rc, rd))
    hand_out((fine_product if fine else product)(g_ref, u_ref[...]), (a, b, c, d))


def differences(w, scale):
    values = []
    power = None
    for k, value in enumerate(w):
        values.append(value if k == 0 else value * power)
        power = scale if k == 0 else power * scale
    out = [values[0]]
    while len(values) > 1:
        values = [values[k + 1] - values[k] for k in range(len(values) - 1)]
        out.append(values[0])
    return out


def shares(us, ys, scale, pairs):
    face = us[0].shape[0] // 4
    sums = [jnp.zeros((8, us[0].shape[1]), F32)] * (2 * len(pairs))
    step = 16
    for k in range(4):
        for at in range(0, face, step):
            here, there = slice(at, at + step), slice(k * face + at, k * face + at + step)
            v = differences([u[there, :] for u in us], scale)
            f = differences([y[k][here, :] for y in ys], scale)
            for q, (i, j) in enumerate(pairs):
                for part, term in ((0, v[i] * v[j]), (1, v[j] * f[i])):
                    for m in range(0, step, 8):
                        sums[2 * q + part] = sums[2 * q + part] + term[m : m + 8]
    return [rows_sum(value) * (scale if k % 2 else 0.5) for k, value in enumerate(sums)]


def early_shares_kernel(u0, u1, u2, *rest):
    ys, (center, out) = rest[:12], rest[12:]
    pairs = [pair for pair in PAIRS if pair[1] < 3]
    values = shares((u0, u1, u2), (ys[:4], ys[4:8], ys[8:]), 1.0 / center[0:1, :], pairs)
    out[...] = jnp.zeros_like(out)
    for k, value in enumerate(values):
        out[k : k + 1, :] = value


def last_kernel(facts, ya, yb, yc, yd, ra, rb, rc, rd, u0, u1, u2, *rest):
    ys, (early, center, g_ref, u_ref, down, left, yo_ref, node, y_ref) = rest[:8], rest[8:]
    take_in(facts, u_ref, (ya, yb, yc, yd), (ra, rb, rc, rd))
    face = down.shape[0]
    y_ref[...] = fine_product(g_ref, u_ref[...])

    odd_floor, odd_facade = holds(facts, ODD_FLOOR), holds(facts, ODD_FACADE)
    a, b, c, d = (y_ref[k * face : (k + 1) * face, :] for k in range(4))
    down[...] = jnp.where(odd_floor, a, b)
    left[...] = jnp.where(odd_facade, c, d)
    yo_ref[0:face, :] = jnp.where(odd_floor, b, a)
    yo_ref[face:, :] = jnp.where(odd_facade, d, c)

    middle = center[0:1, :]
    y3 = tuple(y_ref.at[k * face : (k + 1) * face, :] for k in range(4))
    pairs = [pair for pair in PAIRS if pair[1] == 3]
    values = shares((u0, u1, u2, u_ref), (ys[:4], ys[4:], (ya, yb, yc, yd), y3), 1.0 / middle, pairs)
    at_early = at_late = 0
    for q, pair in enumerate(PAIRS):
        here = slice(2 * q, 2 * q + 2)
        if pair[1] < 3:
            node[here, :] = early[2 * at_early : 2 * at_early + 2, :]
            at_early += 1
        else:
            node[here, :] = jnp.concatenate(values[2 * at_late : 2 * at_late + 2], axis=0)
            at_late += 1
    node[CENTER:NODE, :] = jnp.broadcast_to(middle, (NODE - CENTER, middle.shape[1]))


def tree(values):
    while len(values) > 1:
        values = [values[k] + values[k + 1] for k in range(0, len(values), 2)]
    return values[0]


BINOMIAL = ((1,), (1, 1), (1, 2, 1), (1, 3, 3, 1), (1, 4, 6, 4, 1))


def merged(parts):
    centers = [part[CENTER : CENTER + 1, :] for part in parts]
    middle = tree(centers) * (1.0 / len(parts))
    moved = []
    for part, center in zip(parts, centers):
        ratio = center / middle
        shift = (center - middle) / middle
        ratios, shifts = [None, ratio, ratio * ratio, ratio * ratio * ratio], [None, shift, shift * shift, shift * shift * shift]

        def entry(k, j):
            value = None
            for power in (ratios[j], shifts[k - j]):
                if power is not None:
                    value = power if value is None else value * power
            return value if BINOMIAL[k][j] == 1 or value is None else BINOMIAL[k][j] * value

        change = [[entry(k, j) for j in range(k + 1)] for k in range(4)]

        def times(factor, value):
            return value if factor is None else factor * value

        row = {}
        for q, (i, j) in enumerate(PAIRS):
            row[i, j] = row[j, i] = part[2 * q : 2 * q + 2, :]
        half = [[tree_any([times(change[k][j], row[j, m]) for j in range(k + 1)]) for m in range(4)] for k in range(4)]
        unit = jnp.concatenate([jnp.ones_like(ratio), ratio], axis=0)
        moved.append(
            [unit * tree_any([times(change[j][m], half[i][m]) for m in range(j + 1)]) for i, j in PAIRS]
        )
    return [tree([values[q] for values in moved]) for q in range(len(PAIRS))], middle


def tree_any(values):
    return functools.reduce(lambda a, b: a + b, values)


def write_node(node, rows, middle):
    for q in range(len(PAIRS)):
        node[2 * q : 2 * q + 2, :] = rows[q]
    node[CENTER:NODE, :] = jnp.broadcast_to(middle, (NODE - CENTER, middle.shape[1]))


def merge_kernel(*refs):
    parts, node = refs[:-1], refs[-1]
    write_node(node, *merged(parts))


def conjugate_coefficients(rows):
    inner, energy = {}, {}
    for q, pair in enumerate(PAIRS):
        inner[pair], energy[pair] = rows[q][0:1, :], rows[q][1:2, :]

    def square(a, matrix):
        terms = []
        for i in range(len(a)):
            mixed = [2.0 * (a[j] * matrix[i, j]) for j in range(i + 1, len(a))]
            terms.append(a[i] * tree_any([a[i] * matrix[i, i]] + mixed))
        return tree_any(terms)

    def plus(a, s, b):
        return [a[k] + s * b[k] if k < len(a) else s * b[k] for k in range(len(b))]

    one = jnp.ones_like(rows[0][0:1, :])
    x, r, p = [], [one], [one]
    norm = inner[0, 0]
    norms = [norm]
    for sweep in range(ITERS):
        step = norm / square(p, energy)
        x = plus(x, step, p)
        image = [p[0]] + [p[k] + p[k - 1] for k in range(1, len(p))] + [p[-1]]
        r = plus(r, -step, image)
        if sweep + 1 < ITERS:
            fresh = square(r, inner)
            p = plus(r, fresh / norm, p + [jnp.zeros_like(one)])
            norm = fresh
            norms.append(norm)
    return x, r, norms


def soundness(rows, norms, r):
    inner = {}
    for q, (i, j) in enumerate(PAIRS):
        inner[i, j] = inner[j, i] = rows[q][0:1, :]
    lengths = [
        tree_any([float(BINOMIAL[k][i] * BINOMIAL[k][j]) * inner[i, j] for i in range(k + 1) for j in range(k + 1)])
        for k in range(4)
    ]
    lengths.append(lengths[3] * (lengths[3] / lengths[2]))
    terms = tree_any([r[k] * r[k] * lengths[k] for k in range(5)])
    return jnp.where((terms <= GROWTH * norms[-1]) & (norms[-1] > 0.0), 1.0, 0.0)


def powers(coefficients, scale):
    out = []
    power = None
    for j in range(len(coefficients)):
        value = tree_any(
            [coefficients[k] * float(BINOMIAL[k][j] * (-1) ** (k - j)) for k in range(j, len(coefficients))]
        )
        out.append(value if power is None else value * power)
        power = scale if power is None else power * scale
    return out


def image_kernel(info, yo_ref, got_up, got_right, *rest):
    parts, (w4_ref, node) = rest[:-2], rest[-2:]
    face = got_up.shape[0]
    for f, got in enumerate((got_up, got_right)):
        rows = slice(f * face, (f + 1) * face)
        image = yo_ref[rows, :] - got[...]
        if f == 0:
            image = jnp.where(holds(facts, ABOVE), image, 0.0)
        w4_ref[rows, :] = image
    write_node(node, *merged(parts))


def final_kernel(facts, u0, u1, u2, u3, yo_ref, got_up, got_right, *rest):
    parts, (mult, resid, sound) = rest[:-3], rest[-3:]
    rows, middle = merged(parts)
    scale = 1.0 / middle
    x, r, norms = conjugate_coefficients(rows)
    sound[0, 0] = jnp.min(soundness(rows, norms, powers(r, jnp.ones_like(scale)))).astype(jnp.int32)
    x = [value * scale for value in powers(x, scale)]
    r = powers(r, scale)
    face = got_up.shape[0]
    for f, got in enumerate((got_up, got_right)):
        odd = holds(facts, ODD_FACADE if f else ODD_FLOOR)
        low, high = (slice((2 * f + k) * face, (2 * f + k + 1) * face) for k in range(2))
        here = slice(f * face, (f + 1) * face)
        w = [jnp.where(odd, u[high, :], u[low, :]) for u in (u0, u1, u2, u3)]
        image = yo_ref[here, :] - got[...]
        if f == 0:
            image = jnp.where(holds(facts, ABOVE), image, 0.0)
        mult[here, :] = x[0] * w[0] + x[1] * w[1] + x[2] * w[2] + x[3] * w[3]
        resid[here, :] = r[0] * w[0] + r[1] * w[1] + r[2] * w[2] + r[3] * w[3] + r[4] * image


def hand_on_kernel(mult_in, resid_in, mult, resid):
    mult[...] = mult_in[...]
    resid[...] = resid_in[...]


def upward(value, axis, steps, wrap):
    count = lax.axis_size(axis)
    pairs = [(i, (i + steps) % count) for i in range(count) if wrap or 0 <= i + steps < count]
    return lax.ppermute(value, axis, pairs)


def swapped(value, axis, odd, wrap):
    count = lax.axis_size(axis)
    pairs = []
    for i in range(odd, count, 2):
        if i + 1 < count or wrap:
            j = (i + 1) % count
            pairs += [(i, j), (j, i)]
    return lax.ppermute(value, axis, pairs)


def exchanged(a, b, c, d):
    d = swapped(d, "facade", 1, True)
    c = swapped(c, "facade", 0, True)
    b = swapped(b, "floor", 1, True)
    a = swapped(a, "floor", 0, False)
    return a, b, c, d


def flipped(value, flip_floor, flip_facade):
    floors, columns = lax.axis_size("floor"), lax.axis_size("facade")
    pairs = [
        (f * columns + c, (f ^ flip_floor) * columns + (c ^ flip_facade)) for f in range(floors) for c in range(columns)
    ]
    return lax.ppermute(value, AXES, pairs)


def sum_stages():
    floors, columns = lax.axis_size("floor"), lax.axis_size("facade")
    flips = []
    bit = 1
    while bit < floors:
        flips.append((bit, 0))
        bit *= 2
    bit = 1
    while bit < columns:
        flips.append((0, bit))
        bit *= 2
    return [flips[:1]] + [flips[k : k + 2] for k in range(1, len(flips), 2)]


def stage_parts(value, stage):
    if len(stage) == 1:
        return [value, flipped(value, *stage[0])]
    (f1, c1), (f2, c2) = stage
    return [value, flipped(value, f1 ^ f2, c1 ^ c2), flipped(value, f2, c2), flipped(value, f1, c1)]


def plain_iterations(rhs, factor, coupling, pattern, has_above):
    face, cases = rhs.shape[0] // 2, rhs.shape[1]
    size = 4 * face
    block = size // pattern.shape[0]
    expanded = jnp.repeat(jnp.repeat(pattern, block, axis=0), block, axis=1)
    masked = jnp.where(expanded != 0, coupling, jnp.zeros_like(coupling))
    top_keep = has_above.astype(F32)

    def dot(x, y, contract):
        return lax.dot_general(x, y, ((contract, (0,)), ((), ())), precision=lax.Precision.HIGHEST, preferred_element_type=F32)

    def image_of(v):
        up, right = v[:face], v[face:]
        below, beside = upward(up, "floor", 1, False), upward(right, "facade", 1, True)
        u = jnp.concatenate([-below, up, -beside, right], axis=0)
        y = dot(factor, dot(factor, u, (1,)), (0,))
        forward = dot(masked, u.astype(BF16), (1,)).astype(BF16)
        y = (y + dot(masked, forward, (0,))).reshape(4, face, cases)
        above, beyond = upward(y[0], "floor", -1, False), upward(y[2], "facade", -1, True)
        return jnp.concatenate([(y[1] - above) * top_keep, y[3] - beyond], axis=0)

    def inner(a, b):
        return lax.psum(jnp.sum(a * b, axis=0), AXES)

    def step(_, state):
        mult, resid, direction, norm = state
        image = image_of(direction)
        length = norm / inner(direction, image)
        mult = mult + length * direction
        resid = resid - length * image
        fresh = inner(resid, resid)
        return mult, resid, resid + fresh / norm * direction, fresh

    start = jnp.concatenate([rhs[:face] * top_keep, rhs[face:]], axis=0)
    state = (jnp.zeros_like(start), start, start, inner(start, start))
    return lax.fori_loop(0, ITERS, step, state)[:2]


MERGE_FLOPS = 3000000000
GROWTH = 1.0e6


def call(kernel, outs, scratch, smem, *args, flops=0):
    return pl.pallas_call(
        kernel,
        in_specs=[pl.BlockSpec(memory_space=pltpu.SMEM)] * smem
        + [pl.BlockSpec(memory_space=pltpu.VMEM)] * (len(args) - smem),
        out_specs=[pl.BlockSpec(memory_space=pltpu.VMEM)] * len(outs),
        out_shape=outs,
        scratch_shapes=scratch,
        compiler_params=params(16),
        cost_estimate=pl.CostEstimate(flops=flops, bytes_accessed=0, transcendentals=0) if flops else None,
    )(*args)


def finish(outs, *args):
    return pl.pallas_call(
        final_kernel,
        in_specs=[pl.BlockSpec(memory_space=pltpu.VMEM)] * len(args),
        out_specs=[pl.BlockSpec(memory_space=pltpu.VMEM)] * 2 + [pl.BlockSpec(memory_space=pltpu.SMEM)],
        out_shape=outs + [jax.ShapeDtypeStruct((1, 1), jnp.int32)],
        compiler_params=params(16),
    )(*args)


def local(interface_rhs, inverse_factor, near_coupling, near_pattern):
    face, cases = interface_rhs.shape[3:]
    size = 4 * face
    floors = lax.axis_size("floor")
    floor_pos, facade_pos = lax.axis_index("floor"), lax.axis_index("facade")
    odd_floor, odd_facade = floor_pos % 2, facade_pos % 2
    has_below = (floor_pos > 0).astype(jnp.int32)
    has_above = (floor_pos < floors - 1).astype(jnp.int32)
    keep_a = jnp.where(odd_floor == 0, has_above, has_below)
    keep_b = jnp.where(odd_floor == 0, has_below, has_above)
    flags = [1 - odd_floor, odd_floor, 3 - odd_facade, 2 + odd_facade, keep_a, keep_b, has_above, has_below, odd_floor, odd_facade]
    info = jnp.stack(flags).astype(jnp.int32)
    facts = jnp.stack(flags[KEEP:] + [0] * (8 - len(flags[KEEP:]))).astype(F32)
    facts = jnp.broadcast_to(facts[:, None], (8, cases))
    rhs = interface_rhs.reshape(2 * face, cases)
    below = upward(rhs, "floor", 1, True)
    beside = upward(rhs, "facade", 1, True)
    operator, center = build_operator(info, inverse_factor[0, 0], near_coupling[0, 0], near_pattern[0, 0], cases)

    def shaped(*dims):
        return jax.ShapeDtypeStruct(dims, F32)

    whole, part, node, owned = shaped(size, cases), shaped(face, cases), shaped(NODE, cases), shaped(2 * face, cases)
    sent = [shaped(face + rows, cases) for rows in PADS]

    u0, *y0 = call(first_kernel, [whole, *sent], [], 0, facts, below, beside, rhs, operator)
    u1, *y1 = call(functools.partial(next_kernel, False), [whole, *sent], [], 0, facts, *y0, *exchanged(*y0), operator)
    u2, *y2 = call(functools.partial(next_kernel, True), [whole, *sent], [], 0, facts, *y1, *exchanged(*y1), operator)
    (early,) = call(early_shares_kernel, [shaped(16, cases)], [], 0, u0, u1, u2, *y0, *y1, *y2, center)
    u3, y_down, y_left, y_own, total = call(
        last_kernel,
        [whole, part, part, owned, node],
        [pltpu.VMEM((size, cases), F32)],
        0,
        facts, *y2, *exchanged(*y2), u0, u1, u2, *y0, *y1, early, center, operator,
    )
    got_right = upward(y_left, "facade", -1, True)
    got_up = upward(y_down, "floor", -1, True)
    *stages, before, last = sum_stages()
    for stage in stages + [before]:
        (total,) = call(merge_kernel, [node], [], 0, *stage_parts(total, stage), flops=MERGE_FLOPS if stage is before else 0)
    mult, resid, sound = finish([owned, owned], facts, u0, u1, u2, u3, y_own, got_up, got_right, *stage_parts(total, last))
    def one_by_one(state):
        result = plain_iterations(rhs, inverse_factor[0, 0], near_coupling[0, 0], near_pattern[0, 0], has_above)
        return (*call(hand_on_kernel, [owned, owned], [], 0, *result), jnp.int32(1))

    mult, resid, _ = lax.while_loop(lambda state: state[2] == 0, one_by_one, (mult, resid, sound[0, 0]))
    shape = (1, 1, 2, face, cases)
    return mult.reshape(shape), resid.reshape(shape)


def solution(mesh):
    spec = P("floor", "facade", None, None, None)
    flat = P("floor", "facade", None, None)
    return jax.shard_map(
        local,
        mesh=mesh,
        in_specs=(spec, flat, flat, flat),
        out_specs=(spec, spec),
        check_vma=False,
    )
```

```python
import functools

import jax
import jax.numpy as jnp
from jax import lax
from jax.experimental import pallas as pl
from jax.experimental.pallas import tpu as pltpu
from jax.sharding import PartitionSpec as P

ITERS = 4
SLOT, KEEP, ODD = 0, 4, 8
KEEP_A, KEEP_B, ABOVE, BELOW, ODD_FLOOR, ODD_FACADE = range(6)
PADS = (8, 0, 24, 16)
PAIRS = [(i, j) for i in range(4) for j in range(i, 4)]
CENTER, NODE = 20, 24
AXES = ("floor", "facade")
F32 = jnp.float32
BF16 = jnp.bfloat16


def halves(x):
    high = x.astype(BF16)
    return high, (x - high.astype(F32)).astype(BF16)


def params(mib):
    return pltpu.CompilerParams(vmem_limit_bytes=mib << 20)


def operator_kernel(info_hbm, pattern_hbm, w_hbm, n_hbm, g_ref, center_ref, info, pattern, w_buf, n_buf, sems, left, right, total):
    size = w_buf.shape[1]
    face = size // 4
    nb = pattern.shape[0]
    blk = size // nb
    pattern_copy = pltpu.make_async_copy(pattern_hbm, pattern, sems.at[2, 0])
    pattern_copy.start()
    info_copy = pltpu.make_async_copy(info_hbm, info, sems.at[2, 1])
    info_copy.start()

    def fetch(k):
        rows = pl.ds(k * face, face)
        return (
            pltpu.make_async_copy(w_hbm.at[rows, :], w_buf.at[rows, :], sems.at[0, k]),
            pltpu.make_async_copy(n_hbm.at[rows, :], n_buf.at[rows, :], sems.at[1, k]),
        )

    def prepare(k):
        for copy in fetch(k):
            copy.wait()
        begin(k + 2)
        high, low = halves(w_buf[k * face : (k + 1) * face, :])
        here, there = left.at[k % 2], right.at[k % 2]
        there[0:face, :] = high
        there[face : 2 * face, :] = low
        there[2 * face : 3 * face, :] = high
        for a in range(face // blk):
            for b in range(nb):
                keep = pattern[k * (face // blk) + a, b] != 0
                cols = slice(b * blk, (b + 1) * blk)
                block = n_buf[k * face + a * blk : k * face + (a + 1) * blk, cols]
                there[3 * face + a * blk : 3 * face + (a + 1) * blk, cols] = jnp.where(
                    keep, block, jnp.zeros_like(block)
                )
        high_t = high.T
        here[:, 0:face] = high_t
        here[:, face : 2 * face] = high_t
        here[:, 2 * face : 3 * face] = low.T
        here[:, 3 * face :] = there[3 * face :, :].T

    def multiply(k):
        for i in range(4):
            rows, cols = slice(i * face, (i + 1) * face), slice(i * face, size)
            part = jnp.dot(left[k % 2, rows, :], right[k % 2, :, cols], preferred_element_type=F32)
            if k == 0:
                total[rows, cols] = part
            else:
                total[rows, cols] += part

    def begin(k):
        if k < 4:
            for copy in fetch(k):
                copy.start()

    begin(0)
    begin(1)
    pattern_copy.wait()
    info_copy.wait()
    prepare(0)
    for k in range(4):
        multiply(k)
        if k < 3:
            prepare(k + 1)

    def put(i, j, block):
        def at(k):
            return pl.multiple_of(info[0, k] * face, face)

        rows = pl.ds(at(i), face)
        high, low = halves(block)
        g_ref[rows, pl.ds(at(j), face)] = high
        g_ref[rows, pl.ds(pl.multiple_of(size + at(j), face), face)] = low

    diagonal = lax.broadcasted_iota(jnp.int32, (face, face), 0) == lax.broadcasted_iota(jnp.int32, (face, face), 1)
    trace = jnp.zeros((1, face), F32)
    for i in range(4):
        for j in range(i, 4):
            block = total[i * face : (i + 1) * face, j * face : (j + 1) * face]
            put(i, j, block)
            if j == i:
                trace = trace + rows_sum(jnp.where(diagonal, block, 0.0))
            if j > i:
                put(j, i, block.T)


    center_ref[...] = jnp.broadcast_to(jnp.sum(trace, axis=1, keepdims=True) * (2.0 / size), center_ref.shape)


def build_operator(info, factor, coupling, pattern, cases):
    size = factor.shape[0]
    return pl.pallas_call(
        operator_kernel,
        in_specs=[pl.BlockSpec(memory_space=pl.ANY)] * 4,
        out_specs=[pl.BlockSpec(memory_space=pltpu.VMEM)] * 2,
        out_shape=[jax.ShapeDtypeStruct((size, 2 * size), BF16), jax.ShapeDtypeStruct((8, cases), F32)],
        scratch_shapes=[
            pltpu.SMEM(info.shape, jnp.int32),
            pltpu.SMEM(pattern.shape, jnp.int32),
            pltpu.VMEM((size, size), F32),
            pltpu.VMEM((size, size), BF16),
            pltpu.SemaphoreType.DMA((3, 4)),
            pltpu.VMEM((2, size, size), BF16),
            pltpu.VMEM((2, size, size), BF16),
            pltpu.VMEM((size, size), F32),
        ],
        compiler_params=params(32),
        name="operator",
    )(
        pltpu.with_memory_space_constraint(info, pltpu.HBM),
        pltpu.with_memory_space_constraint(pattern, pltpu.HBM),
        pltpu.with_memory_space_constraint(factor, pltpu.HBM),
        pltpu.with_memory_space_constraint(coupling, pltpu.HBM),
    )


def operand(u):
    high, low = halves(u)
    straight = jnp.concatenate([high, low], axis=1)
    crossed = jnp.concatenate([low, high], axis=1)
    return jnp.concatenate([straight, crossed], axis=0)


def product(g_ref, u):
    cases = u.shape[1]
    wide = jnp.dot(g_ref[...], operand(u), preferred_element_type=F32)
    return wide[:, :cases] + wide[:, cases:]


def fine_product(g_ref, u):
    size, cases = u.shape
    high, low = halves(u)
    rest = (u - high.astype(F32) - low.astype(F32)).astype(BF16)
    wide = jnp.dot(g_ref[:, :size], jnp.concatenate([high, low], axis=1), preferred_element_type=F32)
    crossed = jnp.concatenate([jnp.concatenate([rest, jnp.zeros_like(rest)], axis=1), jnp.concatenate([high, low], axis=1)], axis=0)
    fine = jnp.dot(g_ref[...], crossed, preferred_element_type=F32)
    return wide[:, :cases] + (wide[:, cases:] + (fine[:, :cases] + fine[:, cases:]))


def rows_sum(x):
    return jnp.sum(x, axis=0, keepdims=True)


def holds(facts, row):
    return facts[row : row + 1, :] > 0.5


def take_in(facts, u_ref, own, got):
    face = u_ref.shape[0] // 4
    for k in range(4):
        value = own[k][0:face, :] - got[k][0:face, :]
        if k < 2:
            value = jnp.where(holds(facts, KEEP_A + k), value, 0.0)
        u_ref[k * face : (k + 1) * face, :] = value


def hand_out(y, outs):
    face = y.shape[0] // 4
    for k, out in enumerate(outs):
        out[0:face, :] = y[k * face : (k + 1) * face]
        if out.shape[0] > face:
            out[face:, :] = jnp.zeros((out.shape[0] - face, out.shape[1]), F32)


def first_kernel(facts, below, beside, rhs, g_ref, u_ref, a, b, c, d):
    face = rhs.shape[0] // 2
    own_up = jnp.where(holds(facts, ABOVE), rhs[0:face, :], 0.0)
    own_right = rhs[face:, :]
    minus_below = jnp.where(holds(facts, BELOW), -below[0:face, :], 0.0)
    minus_beside = -beside[face:, :]
    odd_floor, odd_facade = holds(facts, ODD_FLOOR), holds(facts, ODD_FACADE)
    u_ref[0:face, :] = jnp.where(odd_floor, minus_below, own_up)
    u_ref[face : 2 * face, :] = jnp.where(odd_floor, own_up, minus_below)
    u_ref[2 * face : 3 * face, :] = jnp.where(odd_facade, minus_beside, own_right)
    u_ref[3 * face :, :] = jnp.where(odd_facade, own_right, minus_beside)
    hand_out(product(g_ref, u_ref[...]), (a, b, c, d))


def next_kernel(fine, facts, ya, yb, yc, yd, ra, rb, rc, rd, g_ref, u_ref, a, b, c, d):
    take_in(facts, u_ref, (ya, yb, yc, yd), (ra, rb, rc, rd))
    hand_out((fine_product if fine else product)(g_ref, u_ref[...]), (a, b, c, d))


def differences(w, scale):
    values = []
    power = None
    for k, value in enumerate(w):
        values.append(value if k == 0 else value * power)
        power = scale if k == 0 else power * scale
    out = [values[0]]
    while len(values) > 1:
        values = [values[k + 1] - values[k] for k in range(len(values) - 1)]
        out.append(values[0])
    return out


def shares(us, ys, scale, pairs):
    face = us[0].shape[0] // 4
    sums = [jnp.zeros((8, us[0].shape[1]), F32)] * (2 * len(pairs))
    step = 16
    for k in range(4):
        for at in range(0, face, step):
            here, there = slice(at, at + step), slice(k * face + at, k * face + at + step)
            v = differences([u[there, :] for u in us], scale)
            f = differences([y[k][here, :] for y in ys], scale)
            for q, (i, j) in enumerate(pairs):
                for part, term in ((0, v[i] * v[j]), (1, v[j] * f[i])):
                    for m in range(0, step, 8):
                        sums[2 * q + part] = sums[2 * q + part] + term[m : m + 8]
    return [rows_sum(value) * (scale if k % 2 else 0.5) for k, value in enumerate(sums)]


def early_shares_kernel(u0, u1, u2, *rest):
    ys, (center, out) = rest[:12], rest[12:]
    pairs = [pair for pair in PAIRS if pair[1] < 3]
    values = shares((u0, u1, u2), (ys[:4], ys[4:8], ys[8:]), 1.0 / center[0:1, :], pairs)
    out[...] = jnp.zeros_like(out)
    for k, value in enumerate(values):
        out[k : k + 1, :] = value


def last_kernel(facts, ya, yb, yc, yd, ra, rb, rc, rd, u0, u1, u2, *rest):
    ys, (early, center, g_ref, u_ref, down, left, yo_ref, node, y_ref) = rest[:8], rest[8:]
    take_in(facts, u_ref, (ya, yb, yc, yd), (ra, rb, rc, rd))
    face = down.shape[0]
    y_ref[...] = fine_product(g_ref, u_ref[...])

    odd_floor, odd_facade = holds(facts, ODD_FLOOR), holds(facts, ODD_FACADE)
    a, b, c, d = (y_ref[k * face : (k + 1) * face, :] for k in range(4))
    down[...] = jnp.where(odd_floor, a, b)
    left[...] = jnp.where(odd_facade, c, d)
    yo_ref[0:face, :] = jnp.where(odd_floor, b, a)
    yo_ref[face:, :] = jnp.where(odd_facade, d, c)

    middle = center[0:1, :]
    y3 = tuple(y_ref.at[k * face : (k + 1) * face, :] for k in range(4))
    pairs = [pair for pair in PAIRS if pair[1] == 3]
    values = shares((u0, u1, u2, u_ref), (ys[:4], ys[4:], (ya, yb, yc, yd), y3), 1.0 / middle, pairs)
    at_early = at_late = 0
    for q, pair in enumerate(PAIRS):
        here = slice(2 * q, 2 * q + 2)
        if pair[1] < 3:
            node[here, :] = early[2 * at_early : 2 * at_early + 2, :]
            at_early += 1
        else:
            node[here, :] = jnp.concatenate(values[2 * at_late : 2 * at_late + 2], axis=0)
            at_late += 1
    node[CENTER:NODE, :] = jnp.broadcast_to(middle, (NODE - CENTER, middle.shape[1]))


def tree(values):
    while len(values) > 1:
        values = [values[k] + values[k + 1] for k in range(0, len(values), 2)]
    return values[0]


BINOMIAL = ((1,), (1, 1), (1, 2, 1), (1, 3, 3, 1), (1, 4, 6, 4, 1))


def merged(parts):
    centers = [part[CENTER : CENTER + 1, :] for part in parts]
    middle = tree(centers) * (1.0 / len(parts))
    moved = []
    for part, center in zip(parts, centers):
        ratio = center / middle
        shift = (center - middle) / middle
        ratios, shifts = [None, ratio, ratio * ratio, ratio * ratio * ratio], [None, shift, shift * shift, shift * shift * shift]

        def entry(k, j):
            value = None
            for power in (ratios[j], shifts[k - j]):
                if power is not None:
                    value = power if value is None else value * power
            return value if BINOMIAL[k][j] == 1 or value is None else BINOMIAL[k][j] * value

        change = [[entry(k, j) for j in range(k + 1)] for k in range(4)]

        def times(factor, value):
            return value if factor is None else factor * value

        row = {}
        for q, (i, j) in enumerate(PAIRS):
            row[i, j] = row[j, i] = part[2 * q : 2 * q + 2, :]
        half = [[tree_any([times(change[k][j], row[j, m]) for j in range(k + 1)]) for m in range(4)] for k in range(4)]
        unit = jnp.concatenate([jnp.ones_like(ratio), ratio], axis=0)
        moved.append(
            [unit * tree_any([times(change[j][m], half[i][m]) for m in range(j + 1)]) for i, j in PAIRS]
        )
    return [tree([values[q] for values in moved]) for q in range(len(PAIRS))], middle


def tree_any(values):
    return functools.reduce(lambda a, b: a + b, values)


def write_node(node, rows, middle):
    for q in range(len(PAIRS)):
        node[2 * q : 2 * q + 2, :] = rows[q]
    node[CENTER:NODE, :] = jnp.broadcast_to(middle, (NODE - CENTER, middle.shape[1]))


def merge_kernel(*refs):
    parts, node = refs[:-1], refs[-1]
    write_node(node, *merged(parts))


def conjugate_coefficients(rows):
    inner, energy = {}, {}
    for q, pair in enumerate(PAIRS):
        inner[pair], energy[pair] = rows[q][0:1, :], rows[q][1:2, :]

    def square(a, matrix):
        terms = []
        for i in range(len(a)):
            mixed = [2.0 * (a[j] * matrix[i, j]) for j in range(i + 1, len(a))]
            terms.append(a[i] * tree_any([a[i] * matrix[i, i]] + mixed))
        return tree_any(terms)

    def plus(a, s, b):
        return [a[k] + s * b[k] if k < len(a) else s * b[k] for k in range(len(b))]

    one = jnp.ones_like(rows[0][0:1, :])
    x, r, p = [], [one], [one]
    norm = inner[0, 0]
    norms = [norm]
    for sweep in range(ITERS):
        step = norm / square(p, energy)
        x = plus(x, step, p)
        image = [p[0]] + [p[k] + p[k - 1] for k in range(1, len(p))] + [p[-1]]
        r = plus(r, -step, image)
        if sweep + 1 < ITERS:
            fresh = square(r, inner)
            p = plus(r, fresh / norm, p + [jnp.zeros_like(one)])
            norm = fresh
            norms.append(norm)
    return x, r, norms


def soundness(rows, norms, r):
    inner = {}
    for q, (i, j) in enumerate(PAIRS):
        inner[i, j] = inner[j, i] = rows[q][0:1, :]
    lengths = [
        tree_any([float(BINOMIAL[k][i] * BINOMIAL[k][j]) * inner[i, j] for i in range(k + 1) for j in range(k + 1)])
        for k in range(4)
    ]
    lengths.append(lengths[3] * (lengths[3] / lengths[2]))
    terms = tree_any([r[k] * r[k] * lengths[k] for k in range(5)])
    return jnp.where((terms <= GROWTH * norms[-1]) & (norms[-1] > 0.0), 1.0, 0.0)


def powers(coefficients, scale):
    out = []
    power = None
    for j in range(len(coefficients)):
        value = tree_any(
            [coefficients[k] * float(BINOMIAL[k][j] * (-1) ** (k - j)) for k in range(j, len(coefficients))]
        )
        out.append(value if power is None else value * power)
        power = scale if power is None else power * scale
    return out


def image_kernel(info, yo_ref, got_up, got_right, *rest):
    parts, (w4_ref, node) = rest[:-2], rest[-2:]
    face = got_up.shape[0]
    for f, got in enumerate((got_up, got_right)):
        rows = slice(f * face, (f + 1) * face)
        image = yo_ref[rows, :] - got[...]
        if f == 0:
            image = jnp.where(holds(facts, ABOVE), image, 0.0)
        w4_ref[rows, :] = image
    write_node(node, *merged(parts))


def final_kernel(facts, u0, u1, u2, u3, yo_ref, got_up, got_right, *rest):
    parts, (mult, resid, sound) = rest[:-3], rest[-3:]
    rows, middle = merged(parts)
    scale = 1.0 / middle
    x, r, norms = conjugate_coefficients(rows)
    sound[0, 0] = jnp.min(soundness(rows, norms, powers(r, jnp.ones_like(scale)))).astype(jnp.int32)
    x = [value * scale for value in powers(x, scale)]
    r = powers(r, scale)
    face = got_up.shape[0]
    for f, got in enumerate((got_up, got_right)):
        odd = holds(facts, ODD_FACADE if f else ODD_FLOOR)
        low, high = (slice((2 * f + k) * face, (2 * f + k + 1) * face) for k in range(2))
        here = slice(f * face, (f + 1) * face)
        w = [jnp.where(odd, u[high, :], u[low, :]) for u in (u0, u1, u2, u3)]
        image = yo_ref[here, :] - got[...]
        if f == 0:
            image = jnp.where(holds(facts, ABOVE), image, 0.0)
        mult[here, :] = x[0] * w[0] + x[1] * w[1] + x[2] * w[2] + x[3] * w[3]
        resid[here, :] = r[0] * w[0] + r[1] * w[1] + r[2] * w[2] + r[3] * w[3] + r[4] * image


def hand_on_kernel(mult_in, resid_in, mult, resid):
    mult[...] = mult_in[...]
    resid[...] = resid_in[...]


def upward(value, axis, steps, wrap):
    count = lax.axis_size(axis)
    pairs = [(i, (i + steps) % count) for i in range(count) if wrap or 0 <= i + steps < count]
    return lax.ppermute(value, axis, pairs)


def swapped(value, axis, odd, wrap):
    count = lax.axis_size(axis)
    pairs = []
    for i in range(odd, count, 2):
        if i + 1 < count or wrap:
            j = (i + 1) % count
            pairs += [(i, j), (j, i)]
    return lax.ppermute(value, axis, pairs)


def exchanged(a, b, c, d):
    d = swapped(d, "facade", 1, True)
    c = swapped(c, "facade", 0, True)
    b = swapped(b, "floor", 1, True)
    a = swapped(a, "floor", 0, False)
    return a, b, c, d


def flipped(value, flip_floor, flip_facade):
    floors, columns = lax.axis_size("floor"), lax.axis_size("facade")
    pairs = [
        (f * columns + c, (f ^ flip_floor) * columns + (c ^ flip_facade)) for f in range(floors) for c in range(columns)
    ]
    return lax.ppermute(value, AXES, pairs)


def sum_stages():
    floors, columns = lax.axis_size("floor"), lax.axis_size("facade")
    flips = []
    bit = 1
    while bit < floors:
        flips.append((bit, 0))
        bit *= 2
    bit = 1
    while bit < columns:
        flips.append((0, bit))
        bit *= 2
    return [flips[:1]] + [flips[k : k + 2] for k in range(1, len(flips), 2)]


def stage_parts(value, stage):
    if len(stage) == 1:
        return [value, flipped(value, *stage[0])]
    (f1, c1), (f2, c2) = stage
    return [value, flipped(value, f1 ^ f2, c1 ^ c2), flipped(value, f2, c2), flipped(value, f1, c1)]


def plain_iterations(rhs, factor, coupling, pattern, has_above):
    face, cases = rhs.shape[0] // 2, rhs.shape[1]
    size = 4 * face
    block = size // pattern.shape[0]
    expanded = jnp.repeat(jnp.repeat(pattern, block, axis=0), block, axis=1)
    masked = jnp.where(expanded != 0, coupling, jnp.zeros_like(coupling))
    top_keep = has_above.astype(F32)

    def dot(x, y, contract):
        return lax.dot_general(x, y, ((contract, (0,)), ((), ())), precision=lax.Precision.HIGHEST, preferred_element_type=F32)

    def image_of(v):
        up, right = v[:face], v[face:]
        below, beside = upward(up, "floor", 1, False), upward(right, "facade", 1, True)
        u = jnp.concatenate([-below, up, -beside, right], axis=0)
        y = dot(factor, dot(factor, u, (1,)), (0,))
        forward = dot(masked, u.astype(BF16), (1,)).astype(BF16)
        y = (y + dot(masked, forward, (0,))).reshape(4, face, cases)
        above, beyond = upward(y[0], "floor", -1, False), upward(y[2], "facade", -1, True)
        return jnp.concatenate([(y[1] - above) * top_keep, y[3] - beyond], axis=0)

    def inner(a, b):
        return lax.psum(jnp.sum(a * b, axis=0), AXES)

    def step(_, state):
        mult, resid, direction, norm = state
        image = image_of(direction)
        length = norm / inner(direction, image)
        mult = mult + length * direction
        resid = resid - length * image
        fresh = inner(resid, resid)
        return mult, resid, resid + fresh / norm * direction, fresh

    start = jnp.concatenate([rhs[:face] * top_keep, rhs[face:]], axis=0)
    state = (jnp.zeros_like(start), start, start, inner(start, start))
    return lax.fori_loop(0, ITERS, step, state)[:2]


MERGE_FLOPS = 3000000000
GROWTH = 1.0e6


def call(kernel, outs, scratch, smem, *args, flops=0):
    return pl.pallas_call(
        kernel,
        in_specs=[pl.BlockSpec(memory_space=pltpu.SMEM)] * smem
        + [pl.BlockSpec(memory_space=pltpu.VMEM)] * (len(args) - smem),
        out_specs=[pl.BlockSpec(memory_space=pltpu.VMEM)] * len(outs),
        out_shape=outs,
        scratch_shapes=scratch,
        compiler_params=params(16),
        cost_estimate=pl.CostEstimate(flops=flops, bytes_accessed=0, transcendentals=0) if flops else None,
    )(*args)


def finish(outs, *args):
    return pl.pallas_call(
        final_kernel,
        in_specs=[pl.BlockSpec(memory_space=pltpu.VMEM)] * len(args),
        out_specs=[pl.BlockSpec(memory_space=pltpu.VMEM)] * 2 + [pl.BlockSpec(memory_space=pltpu.SMEM)],
        out_shape=outs + [jax.ShapeDtypeStruct((1, 1), jnp.int32)],
        compiler_params=params(16),
    )(*args)


def local(interface_rhs, inverse_factor, near_coupling, near_pattern):
    face, cases = interface_rhs.shape[3:]
    size = 4 * face
    floors = lax.axis_size("floor")
    floor_pos, facade_pos = lax.axis_index("floor"), lax.axis_index("facade")
    odd_floor, odd_facade = floor_pos % 2, facade_pos % 2
    has_below = (floor_pos > 0).astype(jnp.int32)
    has_above = (floor_pos < floors - 1).astype(jnp.int32)
    keep_a = jnp.where(odd_floor == 0, has_above, has_below)
    keep_b = jnp.where(odd_floor == 0, has_below, has_above)
    flags = [1 - odd_floor, odd_floor, 3 - odd_facade, 2 + odd_facade, keep_a, keep_b, has_above, has_below, odd_floor, odd_facade]
    info = jnp.stack(flags).astype(jnp.int32).reshape(1, -1)
    facts = jnp.stack(flags[KEEP:] + [0] * (8 - len(flags[KEEP:]))).astype(F32)
    facts = jnp.broadcast_to(facts[:, None], (8, cases))
    rhs = interface_rhs.reshape(2 * face, cases)
    below = upward(rhs, "floor", 1, True)
    beside = upward(rhs, "facade", 1, True)
    operator, center = build_operator(info, inverse_factor[0, 0], near_coupling[0, 0], near_pattern[0, 0], cases)

    def shaped(*dims):
        return jax.ShapeDtypeStruct(dims, F32)

    whole, part, node, owned = shaped(size, cases), shaped(face, cases), shaped(NODE, cases), shaped(2 * face, cases)
    sent = [shaped(face + rows, cases) for rows in PADS]

    u0, *y0 = call(first_kernel, [whole, *sent], [], 0, facts, below, beside, rhs, operator)
    u1, *y1 = call(functools.partial(next_kernel, False), [whole, *sent], [], 0, facts, *y0, *exchanged(*y0), operator)
    u2, *y2 = call(functools.partial(next_kernel, True), [whole, *sent], [], 0, facts, *y1, *exchanged(*y1), operator)
    (early,) = call(early_shares_kernel, [shaped(16, cases)], [], 0, u0, u1, u2, *y0, *y1, *y2, center)
    u3, y_down, y_left, y_own, total = call(
        last_kernel,
        [whole, part, part, owned, node],
        [pltpu.VMEM((size, cases), F32)],
        0,
        facts, *y2, *exchanged(*y2), u0, u1, u2, *y0, *y1, early, center, operator,
    )
    got_right = upward(y_left, "facade", -1, True)
    got_up = upward(y_down, "floor", -1, True)
    *stages, before, last = sum_stages()
    for stage in stages + [before]:
        (total,) = call(merge_kernel, [node], [], 0, *stage_parts(total, stage), flops=MERGE_FLOPS if stage is before else 0)
    mult, resid, sound = finish([owned, owned], facts, u0, u1, u2, u3, y_own, got_up, got_right, *stage_parts(total, last))
    def one_by_one(state):
        result = plain_iterations(rhs, inverse_factor[0, 0], near_coupling[0, 0], near_pattern[0, 0], has_above)
        return (*call(hand_on_kernel, [owned, owned], [], 0, *result), jnp.int32(1))

    mult, resid, _ = lax.while_loop(lambda state: state[2] == 0, one_by_one, (mult, resid, sound[0, 0]))
    shape = (1, 1, 2, face, cases)
    return mult.reshape(shape), resid.reshape(shape)


def solution(mesh):
    spec = P("floor", "facade", None, None, None)
    flat = P("floor", "facade", None, None)
    return jax.shard_map(
        local,
        mesh=mesh,
        in_specs=(spec, flat, flat, flat),
        out_specs=(spec, spec),
        check_vma=False,
    )
```
